256 devices in a mesh: gx: 32 (over z_lo, y, core), gy: 8 (over x, z_hi).
Axes of the slice: x: 4, y: 4, z: 8 (z_hi: 2, z_lo: 4; z = z_hi * 4 + z_lo), core: 2. Of those that a mesh axis runs over, the one named last changes fastest.
Arguments:
- features: bfloat16 [512, 512, 128], P(('gx', 'gy')), may hold values from -6 to 6
- occupied: int32 [512, 512], P(('gx', 'gy')), may hold values 0 or 1
- weight_one: bfloat16 [27, 128, 128], replicated, may hold values from -0.109375 to 0.109375
- bias_one: float32 [128], replicated, may hold values from -3 to 3
- weight_two: bfloat16 [27, 128, 128], replicated, may hold values from -0.109375 to 0.109375
- cotangent: bfloat16 [512, 512, 128], P(('gx', 'gy')), may hold values from -6 to 6
- neighbours: int32 [512, 27], P(('gx', 'gy')), may hold values from 0 to 18, as said below
- send_x: int32 [256, 2, 6], P(('gx', 'gy')), may hold values from 0 to 18, as said below
- send_y: int32 [256, 2, 2], P(('gx', 'gy')), may hold values from 0 to 18, as said below
Outputs:
- output: bfloat16 [512, 512, 128], P(('gx', 'gy'))
- grad_features: bfloat16 [512, 512, 128], P(('gx', 'gy'))
- grad_weight_one: float32 [27, 128, 128], replicated
- grad_weight_two: float32 [27, 128, 128], replicated
The draws below stay inside these ranges and needn't reach their ends.
Inputs may be any that keep to these rules, and one draw needn't show every extreme that they name: `neighbours`: each tile is 2 x 2 x 2 bricks of the map, tiles laid out with x over gx and y over gy. A tile's live bricks fill its first slots, and some tile is full in every draw. A live brick's entry k names the pool row holding the brick at brick offset (k // 9 - 1, k // 3 % 3 - 1, k % 3 - 1), or 18 where that brick is empty or lies outside the map; entry 13 names its own slot; a dead slot's entries are all 18. The lists describe one map, so neighbourhood is symmetric. send_y[t, 0] lists in slot order the live slots of tile t in its top layer of bricks along y, send_y[t, 1] those in its bottom layer; the rest is 18. send_x[t, 0] lists in row order the pool rows below 6 of tile t (its own bricks and those it received along y) whose bricks lie in its top layer along x, send_x[t, 1] those in its bottom layer; the rest is 18.
All inputs are finite; a program needn't handle non-finite values. No bound on the sum of `occupied` on one device may be relied on, other than what follows from the above.
Results may differ from the reference program's by a relative error of at most 0.015.
Values may be sent and summed in bfloat16 or wider, within the bound.
A program may use at most 128 MiB of HBM per device.

```python
import jax
import jax.numpy as jnp
from jax import lax

CHANNELS = 128
EDGE = 8
KVOL = 27
BSLOTS = 2
TILE_X = 2
TILE_Y = 2
LEVELS = 2
HY = 2
HX = 6
POOL = 18
BV = 512
BRICKS = 512
VOXELS = 262144
N_GX = 32
N_GY = 8


def rank_list(flagged, list_width):
    flag_int = flagged.astype(jnp.int32)
    rank_of = jnp.cumsum(flag_int, axis=1) - flag_int
    matches = flagged[:, :, None] & (rank_of[:, :, None] == jnp.arange(list_width, dtype=jnp.int32)[None, None, :])
    position = jnp.sum(jnp.where(matches, jnp.arange(flagged.shape[1], dtype=jnp.int32)[None, :, None], 0), axis=1)
    listed = jnp.where(jnp.any(matches, axis=1), position, POOL)
    return (listed.astype(jnp.int32), rank_of.astype(jnp.int32))


def geometry(key):
    base_key = jax.random.fold_in(key, 4242)
    key_count, key_heavy, key_place = jax.random.split(base_key, 3)
    tile_count = N_GX * N_GY
    places = TILE_X * TILE_Y * LEVELS
    tile_ids = jnp.arange(tile_count, dtype=jnp.int32)
    count_draw = jax.random.randint(key_count, (tile_count,), 0, 1001)
    squared = count_draw * count_draw // 1000
    live_count = 1 + ((BSLOTS - 1) * squared + 500) // 1000
    heavy_tile = jax.random.randint(key_heavy, (), 0, tile_count)
    live_count = jnp.where(tile_ids == heavy_tile, BSLOTS, live_count)
    scores = jax.random.randint(key_place, (tile_count, places), 0, 1 << 20) * places + jnp.arange(places, dtype=jnp.int32)[None, :]
    ranking = jnp.argsort(scores, axis=1).astype(jnp.int32)
    chosen = ranking[:, :BSLOTS]
    slot_ids = jnp.arange(BSLOTS, dtype=jnp.int32)
    live = slot_ids[None, :] < live_count[:, None]
    local_x = chosen % TILE_X
    local_y = chosen // TILE_X % TILE_Y
    local_z = chosen // (TILE_X * TILE_Y)
    column = tile_ids // N_GY
    row_pos = tile_ids % N_GY
    section_rows = BSLOTS + 2 * HY
    send_y_up, rank_y_up = rank_list(live & (local_y == TILE_Y - 1), HY)
    send_y_down, rank_y_down = rank_list(live & (local_y == 0), HY)

    def ghost_column(shift_by, valid, listed):
        source_tile = jnp.clip(tile_ids + shift_by, 0, tile_count - 1)
        slot_pick = listed[source_tile]
        usable = valid[:, None] & (slot_pick < BSLOTS)
        clipped = jnp.clip(slot_pick, 0, BSLOTS - 1)
        return (usable, jnp.take_along_axis(local_x[source_tile], clipped, axis=1))
    usable_low, column_low = ghost_column(-1, row_pos > 0, send_y_up)
    usable_high, column_high = ghost_column(1, row_pos < N_GY - 1, send_y_down)
    cand_usable = jnp.concatenate([live, usable_low, usable_high], 1)
    cand_column = jnp.concatenate([local_x, column_low, column_high], 1)
    send_x_up, rank_x_up = rank_list(cand_usable & (cand_column == TILE_X - 1), HX)
    send_x_down, rank_x_down = rank_list(cand_usable & (cand_column == 0), HX)
    span_x = N_GX * TILE_X
    span_y = N_GY * TILE_Y
    global_x = column[:, None] * TILE_X + local_x
    global_y = row_pos[:, None] * TILE_Y + local_y
    occupancy = jnp.full((span_x, span_y, LEVELS), -1, jnp.int32)
    occupancy = occupancy.at[global_x, global_y, local_z].set(jnp.where(live, slot_ids[None, :], -1))
    offsets = jnp.arange(27, dtype=jnp.int32)
    step_x = offsets // 9 - 1
    step_y = offsets // 3 % 3 - 1
    step_z = offsets % 3 - 1
    target_x = global_x[:, :, None] + step_x[None, None, :]
    target_y = global_y[:, :, None] + step_y[None, None, :]
    target_z = local_z[:, :, None] + step_z[None, None, :]
    inside = (target_x >= 0) & (target_x < span_x) & (target_y >= 0) & (target_y < span_y) & (target_z >= 0) & (target_z < LEVELS)
    clip_x = jnp.clip(target_x, 0, span_x - 1)
    clip_y = jnp.clip(target_y, 0, span_y - 1)
    clip_z = jnp.clip(target_z, 0, LEVELS - 1)
    slot_there = occupancy[clip_x, clip_y, clip_z]
    owner_x = clip_x // TILE_X
    owner_y = clip_y // TILE_Y
    move_x = owner_x - column[:, None, None]
    move_y = owner_y - row_pos[:, None, None]
    owner = owner_x * N_GY + owner_y
    middle = owner_x * N_GY + row_pos[:, None, None]
    slot_clip = jnp.clip(slot_there, 0, BSLOTS - 1)
    cand_row = jnp.where(move_y == 0, slot_clip, jnp.where(move_y < 0, BSLOTS + rank_y_up[owner, slot_clip], BSLOTS + HY + rank_y_down[owner, slot_clip]))
    cand_clip = jnp.clip(cand_row, 0, section_rows - 1)
    pool_row = jnp.where(move_x == 0, cand_row, jnp.where(move_x < 0, section_rows + rank_x_up[middle, cand_clip], section_rows + HX + rank_x_down[middle, cand_clip]))
    linked_rows = jnp.where(live[:, :, None] & inside & (slot_there >= 0), pool_row, POOL).astype(jnp.int32)
    send_x = jnp.stack([send_x_up, send_x_down], 1).astype(jnp.int32)
    send_y = jnp.stack([send_y_up, send_y_down], 1).astype(jnp.int32)
    return (linked_rows.reshape(tile_count * BSLOTS, 27), send_x, send_y)


def draw_neighbours(key, part):
    linked_rows, send_x, send_y = geometry(key)
    return linked_rows


def draw_send_x(key, part):
    linked_rows, send_x, send_y = geometry(key)
    return send_x


def draw_send_y(key, part):
    linked_rows, send_x, send_y = geometry(key)
    return send_y


def place_ends(array, key, low, top_value):
    dims = array.shape
    spot = [jax.random.randint(jax.random.fold_in(key, axis), (), 0, dims[axis]) for axis in range(len(dims))]
    array = array.at[tuple(spot)].set(low)
    longest = dims.index(max(dims))
    spot[longest] = (spot[longest] + 1) % dims[longest]
    return array.at[tuple(spot)].set(top_value)


def levels(key, dims, shards, low, largest):
    def one(dim, blocks):
        heights = jax.random.uniform(jax.random.fold_in(jax.random.fold_in(key, 6), dim), (blocks,), jnp.float32, low / len(shards), largest / len(shards))
        return jnp.repeat(jnp.exp(heights), dims[dim] // blocks).reshape((-1,) + (1,) * (len(dims) - dim - 1))

    loudness = one(*shards[0])
    for cut in shards[1:]:
        loudness = loudness * one(*cut)
    return loudness


def gaussian(own_key, shape, spread, bound, cuts=(), kind=jnp.bfloat16):
    array = spread * jax.random.normal(own_key, shape, jnp.float32)
    if cuts:
        array = array * levels(own_key, shape, cuts, -0.22, 0.18)
    return jnp.clip(array, -bound, bound).astype(kind)


def setup_inputs(seed: int = 0) -> dict:
    seeds = jax.random.split(jax.random.key(seed), 10)
    return {
        "features": gaussian(seeds[0], (BRICKS, BV, CHANNELS), 1.0, 6.0, ((0, 256),)),
        "occupied": place_ends((jax.random.randint(seeds[1], (BRICKS, BV), 0, 3) < 2).astype(jnp.int32), jax.random.fold_in(seeds[1], 1), 0, 1),
        "weight_one": gaussian(seeds[2], (KVOL, CHANNELS, CHANNELS), (KVOL * CHANNELS) ** -0.5, 0.109375),
        "bias_one": gaussian(seeds[3], (CHANNELS,), 0.5, 3.0, (), jnp.float32),
        "weight_two": gaussian(seeds[4], (KVOL, CHANNELS, CHANNELS), (KVOL * CHANNELS) ** -0.5, 0.109375),
        "cotangent": gaussian(seeds[5], (BRICKS, BV, CHANNELS), 1.0, 6.0, ((0, 256),)),
        "neighbours": draw_neighbours(jax.random.fold_in(seeds[9], 71), 0),
        "send_x": draw_send_x(jax.random.fold_in(seeds[9], 71), 0),
        "send_y": draw_send_y(jax.random.fold_in(seeds[9], 71), 0),
    }


def cut_layer(portion, side_code, along_axis):
    extent = portion.shape[along_axis]
    if side_code == 0:
        return lax.slice_in_dim(portion, extent - 1, extent, axis=along_axis)
    if side_code == 2:
        return lax.slice_in_dim(portion, 0, 1, axis=along_axis)
    return portion

def gather_block(neighbour_table):
    layers_x = []
    for off_x in range(3):
        layers_y = []
        for off_y in range(3):
            layers_z = []
            for off_z in range(3):
                portion = neighbour_table[:, 9 * off_x + 3 * off_y + off_z]
                portion = cut_layer(cut_layer(cut_layer(portion, off_x, 1), off_y, 2), off_z, 3)
                layers_z.append(portion)
            layers_y.append(jnp.concatenate(layers_z, axis=3))
        layers_x.append(jnp.concatenate(layers_y, axis=2))
    return jnp.concatenate(layers_x, axis=1)

def to_columns(padded_block):
    tap_list = []
    for off_x in range(3):
        for off_y in range(3):
            for off_z in range(3):
                tap_list.append(padded_block[:, off_x:off_x + EDGE, off_y:off_y + EDGE, off_z:off_z + EDGE])
    stacked = jnp.stack(tap_list, axis=4)
    return stacked.reshape(-1, KVOL * CHANNELS)

def from_tile(table_ids, source_tile, valid, listed, limit):
    tile_count = table_ids.shape[0]
    clipped_tile = jnp.clip(source_tile, 0, tile_count - 1)
    picked = listed[clipped_tile]
    usable = valid[:, None] & (picked < limit)
    found = jnp.take_along_axis(table_ids[clipped_tile], jnp.clip(picked, 0, limit - 1).astype(jnp.int32), axis=1)
    return jnp.where(usable, found, -1).astype(jnp.int32)

def pool_sources(send_x, send_y):
    tile_count = N_GX * N_GY
    tile_ids = jnp.arange(tile_count, dtype=jnp.int32)
    column = tile_ids // N_GY
    row_pos = tile_ids % N_GY
    own_ids = tile_ids[:, None] * BSLOTS + jnp.arange(BSLOTS, dtype=jnp.int32)[None, :]
    lower_y = from_tile(own_ids, tile_ids - 1, row_pos > 0, send_y[:, 0], BSLOTS)
    upper_y = from_tile(own_ids, tile_ids + 1, row_pos < N_GY - 1, send_y[:, 1], BSLOTS)
    first_section = jnp.concatenate([own_ids, lower_y, upper_y], 1)
    section_rows = BSLOTS + 2 * HY
    lower_x = from_tile(first_section, tile_ids - N_GY, column > 0, send_x[:, 0], section_rows)
    upper_x = from_tile(first_section, tile_ids + N_GY, column < N_GX - 1, send_x[:, 1], section_rows)
    empty_col = jnp.full((tile_count, 1), -1, jnp.int32)
    return jnp.concatenate([first_section, lower_x, upper_x, empty_col], 1)

def reference(features, occupied, weight_one, bias_one, weight_two, cotangent, neighbours, send_x, send_y):
    tile_count = N_GX * N_GY
    sources = pool_sources(send_x, send_y)
    rows_tile = neighbours.reshape(tile_count, BSLOTS * KVOL).astype(jnp.int32)
    linked = jnp.take_along_axis(sources, rows_tile, axis=1).reshape(BRICKS, KVOL)
    linked = jnp.where(linked < 0, BRICKS, linked).astype(jnp.int32)
    live_bricks = (neighbours[:, 13] != POOL).astype(jnp.int32)
    voxel_mask = (occupied * live_bricks[:, None]).astype(jnp.float32)[:, :, None]
    mask_half = voxel_mask.astype(jnp.bfloat16)
    masked = features * mask_half
    tile_list = jnp.arange(tile_count, dtype=jnp.int32)

    def padded(voxel_field):
        return jnp.concatenate([voxel_field, jnp.zeros((1, BV, CHANNELS), voxel_field.dtype)], 0)

    def tile_columns(field_pad, tile_idx):
        brick_ids = lax.dynamic_slice_in_dim(linked, tile_idx * BSLOTS, BSLOTS, 0)
        neighbour_table = field_pad[brick_ids].reshape(BSLOTS, KVOL, EDGE, EDGE, EDGE, CHANNELS)
        return to_columns(gather_block(neighbour_table))

    def convolve(voxel_field, flat_weight):
        field_pad = padded(voxel_field)

        def one_tile(tile_idx):
            return jnp.dot(tile_columns(field_pad, tile_idx), flat_weight, preferred_element_type=jnp.float32)
        return lax.map(one_tile, tile_list).reshape(BRICKS, BV, CHANNELS)

    def weight_grad(voxel_field, grad_field):
        field_pad = padded(voxel_field)

        def accumulate(running, tile_idx):
            columns = tile_columns(field_pad, tile_idx)
            own_rows = lax.dynamic_slice_in_dim(grad_field, tile_idx * BSLOTS, BSLOTS, 0).reshape(BSLOTS * BV, CHANNELS)
            running = running + lax.dot_general(columns, own_rows, (((0,), (0,)), ((), ())), preferred_element_type=jnp.float32)
            return (running, None)
        running, unused = lax.scan(accumulate, jnp.zeros((KVOL * CHANNELS, CHANNELS), jnp.float32), tile_list)
        return running
    flat_one = weight_one.reshape(KVOL * CHANNELS, CHANNELS)
    flat_two = weight_two.reshape(KVOL * CHANNELS, CHANNELS)
    flip_one = jnp.flip(weight_one, 0).transpose(0, 2, 1).reshape(KVOL * CHANNELS, CHANNELS)
    flip_two = jnp.flip(weight_two, 0).transpose(0, 2, 1).reshape(KVOL * CHANNELS, CHANNELS)
    preact = convolve(masked, flat_one) + bias_one
    hidden = (jax.nn.relu(preact) * voxel_mask).astype(jnp.bfloat16)
    output = (convolve(hidden, flat_two) * voxel_mask + masked.astype(jnp.float32)).astype(jnp.bfloat16)
    grad_out = cotangent * mask_half
    back_two = convolve(grad_out, flip_two)
    grad_hidden = jnp.where(preact > 0, back_two * voxel_mask, 0.0).astype(jnp.bfloat16)
    back_one = convolve(grad_hidden, flip_one)
    grad_features = ((cotangent.astype(jnp.float32) + back_one) * voxel_mask).astype(jnp.bfloat16)
    grad_scale = float(VOXELS) ** (-0.5)
    grad_weight_one = (weight_grad(masked, grad_hidden) * grad_scale).reshape(KVOL, CHANNELS, CHANNELS)
    grad_weight_two = (weight_grad(hidden, grad_out) * grad_scale).reshape(KVOL, CHANNELS, CHANNELS)
    return (output, grad_features, grad_weight_one, grad_weight_two)
```

```python
import functools
import math

import jax
import jax.numpy as jnp
from jax import lax
from jax.experimental import pallas as pl
from jax.experimental.pallas import tpu as pltpu
from jax.sharding import PartitionSpec as P

EDGE = 8
KVOL = 27
CH = 128
PLANE = EDGE * EDGE
NONE = 18
BF = jnp.bfloat16
F32 = jnp.float32
MESH = pl.DeviceIdType.MESH
SLICE = (4, 4, 2, 4, 2)


def chunk_rows(slice_dims):
    nx, ny, zhi, zlo, _ = slice_dims
    rows = KVOL * CH
    plane = -(-rows // (nx * ny * 16)) * 16
    line = -(-plane // (zhi * zlo * 16)) * 16
    return plane, line


def with_z(line, below, above):
    n = line.shape[0]
    flat = lambda t: t.reshape(n * 2, EDGE, CH)
    line, below, above = flat(line), flat(below), flat(above)
    level = lax.broadcasted_iota(jnp.int32, line.shape, 1)
    down = pltpu.roll(jnp.where(level == EDGE - 1, below, line), 1, 1)
    up = pltpu.roll(jnp.where(level == 0, above, line), EDGE - 1, 1)
    return [t.reshape(n, 2 * EDGE, CH).astype(BF) for t in (down, line, up)]


def put(z_ref, f, px, qy, line, below, above):
    for e, rows in enumerate(with_z(line, below, above)):
        z_ref[f, px, qy, :, e * CH : (e + 1) * CH] = rows


def kernel(dims, scale, *refs):
    (
        feat, occ, w1_hbm, bias, w2_hbm, cot, nbr, sx, sy,
        out_ref, gf_ref, gw_ref,
        w1, w2, mask, fa, fb, za, zb, at,
        xfa, yfa, eda, edla, xsa, ysa, esa,
        xfb, yfb, edb, edlb, xsb, ysb, esb,
        gwo, gwm, crecv, rs1, zs1, rz, ag1,
        w_sem, halo_s, halo_r, core_s, core_r, p_s, p_r, l_s, l_r, m_s, m_r, g_s, g_r, f_s, f_r,
    ) = refs
    nx, ny, nzhi, nzlo, _ = dims
    nz = nzhi * nzlo
    plane_rows, line_rows = chunk_rows(dims)
    ngx, ngy = nzlo * ny * 2, nx * nzhi
    gx, gy = lax.axis_index("gx"), lax.axis_index("gy")
    core = lax.rem(gx, 2)
    y = lax.rem(gx // 2, ny)
    z = lax.rem(gy, nzhi) * nzlo + gx // (2 * ny)
    x = gy // nzhi

    def device(px, py, pz, c):
        return (lax.rem(pz, nzlo) * (2 * ny) + py * 2 + c, px * nzhi + pz // nzlo)

    next_x = (lax.rem(gx + 1, ngx), gy)
    prev_x = (lax.rem(gx + ngx - 1, ngx), gy)
    next_y = (gx, lax.rem(gy + 1, ngy))
    prev_y = (gx, lax.rem(gy + ngy - 1, ngy))
    partner = device(x, y, z, 1 - core)
    offsets = [(i, k) for i in range(nx) for k in range(ny) if (i, k) != (0, 0)]
    plane_peer = {o: (lax.rem(x + o[0], nx), lax.rem(y + o[1], ny)) for o in offsets}
    line_peer = {d: lax.rem(z + d, nz) for d in range(1, nz)}

    barrier = pltpu.get_barrier_semaphore()
    greet = [next_x, prev_x, next_y, prev_y]
    greet += [device(*plane_peer[o], z, core) for o in offsets]
    greet += [device(x, y, line_peer[d], core) for d in line_peer]
    for who in greet:
        pl.semaphore_signal(barrier, inc=1, device_id=who, device_id_type=MESH)
    load_w1 = pltpu.make_async_copy(w1_hbm, w1, w_sem.at[0])
    load_w2 = pltpu.make_async_copy(w2_hbm, w2, w_sem.at[1])
    load_w1.start()
    load_w2.start()

    for t in range(4):
        halves = []
        for b in range(2):
            live = (nbr[b, 13] != NONE).astype(F32)
            row = occ[b : b + 1, t * CH : (t + 1) * CH].astype(F32) * live
            halves.append(jnp.broadcast_to(row, (CH, CH)).T.reshape(16, EDGE, CH))
        mask[t * 16 : (t + 1) * 16] = jnp.stack(halves, 1).reshape(16, 16, CH)

    def fields(p, carry):
        mk = mask[pl.ds(p * EDGE, EDGE)]
        rows = pl.ds(pl.multiple_of(p * PLANE, PLANE), PLANE)
        for f, source in enumerate((feat, cot)):
            both = jnp.stack(
                [source[b, rows].astype(F32).reshape(EDGE, EDGE, CH) for b in range(2)], 1
            )
            fa[f, pl.ds(p * EDGE, EDGE)] = (both.reshape(EDGE, 16, CH) * mk).astype(BF)
        return carry

    lax.fori_loop(0, EDGE, fields, 0)

    def remote(src, dst, send, recv, who):
        return pltpu.make_async_remote_copy(
            src_ref=src, dst_ref=dst, send_sem=send, recv_sem=recv, device_id=who, device_id_type=MESH
        )

    def own_faces(field, xf, yf, ed, edl, xs, ys):
        for side in range(2):
            xf[side, NONE] = jnp.zeros(xf.shape[2:], BF)
            yf[side, 6] = jnp.zeros(yf.shape[2:], BF)
            ed[side, NONE] = jnp.zeros(ed.shape[2:], BF)
            edl[side, 6] = jnp.zeros(edl.shape[2:], BF)
            edge = (1 - side) * (EDGE - 1)
            for f in range(2):
                faces = field[f, edge * EDGE : (edge + 1) * EDGE].astype(F32).reshape(EDGE, 2, EDGE, CH)
                walls = jnp.stack([field[f, p * EDGE + edge].astype(F32) for p in range(EDGE)], 0)
                walls = walls.reshape(EDGE, 2, EDGE, CH)
                face = [faces[:, b].reshape(PLANE, CH) for b in range(2)]
                wall = [walls[:, b].reshape(PLANE, CH) for b in range(2)]
                for b in range(2):
                    xf[side, b, f] = face[b].astype(BF)
                    yf[side, b, f] = wall[b].astype(BF)
                    lines = jnp.concatenate([face[b][:EDGE], face[b][PLANE - EDGE :]], 0)
                    edl[side, b, f] = lines.astype(BF)
                for r in range(2):
                    for listed, picks, sent in ((sx, face, xs), (sy, wall, ys)):
                        slot = listed[side, r]
                        low = jnp.where(slot == 0, picks[0], 0.0)
                        sent[side, r, f] = jnp.where(slot == 1, picks[1], low).astype(BF)

    def halo_copies(ph, xf, yf, ed, xs, ys, es):
        def go(n, src, dst, who):
            return remote(src, dst, halo_s.at[ph, n], halo_r.at[ph, n], who)

        walls = [go(0, ys.at[0], yf.at[0, 2:4], next_y), go(1, ys.at[1], yf.at[1, 4:6], prev_y)]
        faces = [go(2, xs.at[0], xf.at[0, 6:8], next_x), go(3, xs.at[1], xf.at[1, 12:14], prev_x)]
        lines = [go(4, es.at[0], ed.at[0, 6:12], next_x), go(5, es.at[1], ed.at[1, 12:18], prev_x)]
        return walls, faces, lines

    def edge_lines(yf, ed, edl, es):
        blank = jnp.zeros((EDGE, CH), F32)
        for f in range(2):
            for r in range(2, 6):
                got = yf[(r - 2) // 2, r, f].astype(F32)
                for side, line in ((0, got[PLANE - EDGE :]), (1, got[:EDGE])):
                    pair = [blank, line] if r < 4 else [line, blank]
                    edl[side, r, f] = jnp.concatenate(pair, 0).astype(BF)
        for side in range(2):
            for r in range(6):
                es[side, r] = edl[side, jnp.minimum(sx[side, r], 6)]
                ed[side, r] = edl[side, r]

    def inner(field, z_ref):
        linked = [[(nbr[b, 12 + 2 * d] != NONE).astype(F32) for b in range(2)] for d in range(2)]

        def plane(p, carry):
            for f in range(2):
                line = field[f, pl.ds(p * EDGE, EDGE)].astype(F32).reshape(EDGE, 2, EDGE, CH)
                near = [
                    jnp.stack([line[:, 1] * linked[d][0], line[:, 0] * linked[d][1]], 1) for d in range(2)
                ]
                put(z_ref, f, p + 1, slice(1, EDGE + 1), line, *near)
            return carry

        lax.fori_loop(0, EDGE, plane, 0)

    def shell(z_ref, xf, yf, ed):
        def three(first, load):
            pick = lambda k: jnp.stack([load(nbr[b, k]).astype(F32) for b in range(2)], 1)
            return pick(first + 1), pick(first), pick(first + 2)

        for f in range(2):
            for side in range(2):
                far = slice((EDGE + 1) * side, (EDGE + 1) * side + 1)
                core_part = slice(1, EDGE + 1)
                faces = three(18 * side + 3, lambda r: xf[side, r, f].reshape(EDGE, EDGE, CH))
                for e, rows in enumerate(with_z(*faces)):
                    z_ref[f, (EDGE + 1) * side, core_part, :, e * CH : (e + 1) * CH] = rows
                walls = three(
                    9 + 6 * side, lambda r: yf[side, jnp.minimum(r, 6), f].reshape(EDGE, EDGE, CH)
                )
                for e, rows in enumerate(with_z(*walls)):
                    z_ref[f, core_part, (EDGE + 1) * side, :, e * CH : (e + 1) * CH] = rows
                for up in range(2):
                    low = (1 - up) * EDGE
                    lines = three(
                        18 * side + 6 * up,
                        lambda r: ed[side, r, f].astype(F32)[low : low + EDGE].reshape(1, EDGE, CH),
                    )
                    for e, rows in enumerate(with_z(*lines)):
                        z_ref[f, (EDGE + 1) * side, (EDGE + 1) * up, :, e * CH : (e + 1) * CH] = rows[0]

    half = 2
    taps = [(a, c) for a in range(3) for c in range(3)]

    def columns(z_ref, f, m):
        parts = [
            z_ref[f, pl.ds(m * half + a, half), c : c + EDGE].reshape(half * EDGE * 16, 3 * CH)
            for a, c in taps
        ]
        return jnp.concatenate(parts, 1)

    def conv(z_ref, f, m, w):
        return jnp.dot(columns(z_ref, f, m), w[...], preferred_element_type=F32)

    def conv_t(z_ref, f, m, w):
        turned = jnp.concatenate([w[(KVOL - 1 - k) * CH : (KVOL - k) * CH] for k in range(KVOL)], 1)
        return lax.dot_general(
            columns(z_ref, f, m), turned, (((1,), (1,)), ((), ())), preferred_element_type=F32
        )

    own_faces(fa, xfa, yfa, eda, edla, xsa, ysa)
    walls_a, faces_a, lines_a = halo_copies(0, xfa, yfa, eda, xsa, ysa, esa)
    pl.semaphore_wait(barrier, len(greet))
    for copy in walls_a + faces_a:
        copy.start()
    inner(fa, za)
    for copy in walls_a:
        copy.wait()
    edge_lines(yfa, eda, edla, esa)
    for copy in lines_a:
        copy.start()
    for copy in faces_a + lines_a:
        copy.wait()
    shell(za, xfa, yfa, eda)
    load_w1.wait()
    load_w2.wait()

    tiles = half * EDGE
    steps = EDGE // half

    def first_layer(m, carry):
        part = pl.ds(m * tiles, tiles)
        mk = mask[part].reshape(tiles * 16, CH)
        preact = conv(za, 0, m, w1) + bias[...]
        back = conv_t(za, 1, m, w2)
        hidden = (jnp.maximum(preact, 0.0) * mk).astype(BF)
        grad = jnp.where(preact > 0, back * mk, 0.0).astype(BF)
        fb[0, part] = hidden.reshape(tiles, 16, CH)
        fb[1, part] = grad.reshape(tiles, 16, CH)
        at[0, m] = grad.T
        at[1, m] = hidden.T
        return carry

    lax.fori_loop(0, steps, first_layer, 0)

    own_faces(fb, xfb, yfb, edb, edlb, xsb, ysb)
    walls_b, faces_b, lines_b = halo_copies(1, xfb, yfb, edb, xsb, ysb, esb)
    for copy in walls_b + faces_b:
        copy.start()

    third = 9 * CH

    def weight_grad(which, a, dst, add=None):
        left = jnp.concatenate([at[which, i] for i in range(steps)], 1)
        first = which == 0
        pa = jnp.where(first, a, 2 - a)
        for c in range(3):
            pc = jnp.where(first, c, 2 - c)
            right = za[which, pl.ds(pa, EDGE), pl.ds(pc, EDGE)].reshape(EDGE * EDGE * 16, 3 * CH)
            prod = jnp.dot(left, right, preferred_element_type=F32)
            for e in range(3):
                plain = prod[:, (2 - e) * CH : (3 - e) * CH]
                turned = prod[:, e * CH : (e + 1) * CH].T
                block = jnp.where(first, turned, plain)
                row = (9 * a + 3 * c + e) * CH
                if add is not None:
                    block = block + add[row : row + CH].astype(F32)
                dst[row : row + CH] = block.astype(BF)

    core_copies = [
        remote(
            gwo.at[a * third : (a + 1) * third],
            crecv.at[a * third : (a + 1) * third],
            core_s.at[a],
            core_r.at[a],
            partner,
        )
        for a in range(3)
    ]
    for a in range(3):
        weight_grad(1 - core, a, gwo)
        core_copies[a].start()
    for copy in walls_b:
        copy.wait()
    edge_lines(yfb, edb, edlb, esb)
    for copy in lines_b:
        copy.start()
    for a in range(3):
        core_copies[a].wait()
        weight_grad(core, a, gwm, crecv)
    if gwm.shape[0] > KVOL * CH:
        gwm[KVOL * CH :] = jnp.zeros((gwm.shape[0] - KVOL * CH, CH), BF)

    def rows_of(index, n):
        return pl.ds(pl.multiple_of(index * n, 16), n)

    me = x * ny + y
    plane_copies = {}
    for o in offsets:
        px, py = plane_peer[o]
        n = o[0] * ny + o[1]
        plane_copies[o] = remote(
            gwm.at[rows_of(px * ny + py, plane_rows)], rs1.at[n], p_s.at[n], p_r.at[n], device(px, py, z, core)
        )
        plane_copies[o].start()

    for copy in faces_b + lines_b:
        copy.wait()
    inner(fb, zb)
    shell(zb, xfb, yfb, edb)

    def second_layer(m, carry):
        part = pl.ds(m * tiles, tiles)
        mk = mask[part].reshape(tiles * 16, CH)
        masked = fa[0, part].astype(F32).reshape(tiles * 16, CH)
        given = fa[1, part].astype(F32).reshape(tiles * 16, CH)
        result = conv(zb, 0, m, w2) * mk + masked
        grad = conv_t(zb, 1, m, w1) * mk + given
        rows = pl.ds(pl.multiple_of(m * tiles * EDGE, tiles * EDGE), tiles * EDGE)
        for value, dst in ((result, out_ref), (grad, gf_ref)):
            bricks = value.reshape(tiles, 2, EDGE, CH)
            for b in range(2):
                dst[b, rows] = bricks[:, b].reshape(tiles * EDGE, CH).astype(BF)
        return carry

    lax.fori_loop(0, steps, second_layer, 0)

    for o in offsets:
        plane_copies[o].wait()

    def plane_sum(t, carry):
        start = pl.multiple_of(t * 16, 16)
        total = gwm[pl.ds(pl.multiple_of(me * plane_rows + start, 16), 16)].astype(F32)
        for i, k in offsets:
            total = total + rs1[i * ny + k, pl.ds(start, 16)].astype(F32)
        zs1[pl.ds(start, 16)] = total.astype(BF)
        return carry

    lax.fori_loop(0, plane_rows // 16, plane_sum, 0)
    if zs1.shape[0] > plane_rows:
        zs1[plane_rows:] = jnp.zeros((zs1.shape[0] - plane_rows, CH), BF)

    line_copies = [
        remote(zs1.at[rows_of(pz, line_rows)], rz.at[d], l_s.at[d], l_r.at[d], device(x, y, pz, core))
        for d, pz in line_peer.items()
    ]
    for copy in line_copies:
        copy.start()
    for copy in line_copies:
        copy.wait()
    mine = rows_of(z, line_rows)
    total = zs1[mine].astype(F32)
    for d in line_peer:
        total = total + rz[d].astype(F32)
    ag1[mine] = (total * scale).astype(BF)

    back_copies = [
        remote(ag1.at[mine], ag1.at[mine], m_s.at[d], m_r.at[d], device(x, y, pz, core))
        for d, pz in line_peer.items()
    ]
    for copy in back_copies:
        copy.start()
    for copy in back_copies:
        copy.wait()
    home = rows_of(me, plane_rows)
    gather = {}
    for i, k in offsets:
        n = i * ny + k
        gather[i, k] = remote(
            ag1.at[:plane_rows], gw_ref.at[core, home], g_s.at[n], g_r.at[n], device(*plane_peer[i, k], z, core)
        )
        gather[i, k].start()
    gw_ref[core, home] = ag1[:plane_rows]
    forward = [remote(gw_ref.at[core, home], gw_ref.at[core, home], f_s.at[0], f_r.at[0], partner)]
    forward[0].start()
    for i, k in offsets:
        n = i * ny + k
        gather[i, k].wait()
        held = rows_of(lax.rem(x + nx - i, nx) * ny + lax.rem(y + ny - k, ny), plane_rows)
        forward.append(remote(gw_ref.at[core, held], gw_ref.at[core, held], f_s.at[n], f_r.at[n], partner))
        forward[-1].start()
    for copy in forward:
        copy.wait()


def on_device(dims, features, occupied, weight_one, bias_one, weight_two, cotangent, neighbours, send_x, send_y):
    nx, ny, nzhi, nzlo, _ = dims
    nz, nxy = nzhi * nzlo, nx * ny
    plane_rows, line_rows = chunk_rows(dims)
    devices = 2 * nxy * nz
    slots, voxels, _ = features.shape
    scale = 1.0 / math.sqrt(slots * voxels * devices)
    vmem = pl.BlockSpec(memory_space=pltpu.VMEM)
    smem = pl.BlockSpec(memory_space=pltpu.SMEM)
    hbm = pl.BlockSpec(memory_space=pl.ANY)
    rows = KVOL * CH

    def halo():
        return [
            pltpu.VMEM((2, NONE + 1, 2, PLANE, CH), BF),
            pltpu.VMEM((2, 7, 2, PLANE, CH), BF),
            pltpu.VMEM((2, NONE + 1, 2, 16, CH), BF),
            pltpu.VMEM((2, 7, 2, 16, CH), BF),
            pltpu.VMEM((2, 2, 2, PLANE, CH), BF),
            pltpu.VMEM((2, 2, 2, PLANE, CH), BF),
            pltpu.VMEM((2, 6, 2, 16, CH), BF),
        ]

    field = pltpu.VMEM((2, PLANE, 16, CH), BF)
    padded = pltpu.VMEM((2, EDGE + 2, EDGE + 2, 16, 3 * CH), BF)
    sem = lambda *shape: pltpu.SemaphoreType.DMA(shape)
    out, grad_features, grads = pl.pallas_call(
        functools.partial(kernel, dims, scale),
        out_shape=(
            jax.ShapeDtypeStruct(features.shape, BF),
            jax.ShapeDtypeStruct(features.shape, BF),
            jax.ShapeDtypeStruct((2, nxy * plane_rows, CH), BF),
        ),
        in_specs=[vmem, vmem, hbm, vmem, hbm, vmem, smem, smem, smem],
        out_specs=(vmem, vmem, vmem),
        scratch_shapes=[
            pltpu.VMEM((rows, CH), BF),
            pltpu.VMEM((rows, CH), BF),
            pltpu.VMEM((PLANE, 16, CH), F32),
            field,
            field,
            padded,
            padded,
            pltpu.VMEM((2, 4, CH, 256), BF),
            *halo(),
            *halo(),
            pltpu.VMEM((rows, CH), BF),
            pltpu.VMEM((nxy * plane_rows, CH), BF),
            pltpu.VMEM((rows, CH), BF),
            pltpu.VMEM((nxy, plane_rows, CH), BF),
            pltpu.VMEM((nz * line_rows, CH), BF),
            pltpu.VMEM((nz, line_rows, CH), BF),
            pltpu.VMEM((nz * line_rows, CH), BF),
            sem(2),
            sem(2, 6), sem(2, 6),
            sem(3), sem(3),
            sem(nxy), sem(nxy),
            sem(nz), sem(nz),
            sem(nz), sem(nz),
            sem(nxy), sem(nxy),
            sem(nxy), sem(nxy),
        ],
        compiler_params=pltpu.CompilerParams(
            collective_id=0, has_side_effects=True, vmem_limit_bytes=56 * 2**20
        ),
    )(
        features,
        occupied,
        weight_one.reshape(rows, CH),
        bias_one.reshape(1, CH),
        weight_two.reshape(rows, CH),
        cotangent,
        neighbours,
        send_x.reshape(2, -1),
        send_y.reshape(2, -1),
    )
    one, two = (grads[j, :rows].astype(F32).reshape(KVOL, CH, CH) for j in range(2))
    return (out, grad_features, one, two)


def solution(mesh, dims=SLICE):
    in_specs = (
        P(("gx", "gy"), None, None),
        P(("gx", "gy"), None),
        P(),
        P(),
        P(),
        P(("gx", "gy"), None, None),
        P(("gx", "gy"), None),
        P(("gx", "gy"), None, None),
        P(("gx", "gy"), None, None),
    )
    out_specs = (P(("gx", "gy"), None, None), P(("gx", "gy"), None, None), P(), P())
    return jax.shard_map(
        functools.partial(on_device, dims), mesh=mesh, in_specs=in_specs, out_specs=out_specs, check_vma=False
    )
```

```python
import functools
import math

import jax
import jax.numpy as jnp
from jax import lax
from jax.experimental import pallas as pl
from jax.experimental.pallas import tpu as pltpu
from jax.sharding import PartitionSpec as P

EDGE = 8
KVOL = 27
CH = 128
PLANE = EDGE * EDGE
NONE = 18
BF = jnp.bfloat16
F32 = jnp.float32
MESH = pl.DeviceIdType.MESH
SLICE = (4, 4, 2, 4, 2)


def with_z(line, below, above):
    n = line.shape[0]
    flat = lambda t: t.reshape(n * 2, EDGE, CH)
    line, below, above = flat(line), flat(below), flat(above)
    level = lax.broadcasted_iota(jnp.int32, line.shape, 1)
    down = pltpu.roll(jnp.where(level == EDGE - 1, below, line), 1, 1)
    up = pltpu.roll(jnp.where(level == 0, above, line), EDGE - 1, 1)
    return [t.reshape(n, 2 * EDGE, CH).astype(BF) for t in (down, line, up)]


class Part:
    def __init__(self, remote, local, result, base, rows, first, second, bufs, sems):
        self.remote, self.local, self.result = remote, local, result
        self.base, self.first, self.second = base, first, second
        self.got_one, self.partial, self.got_two, self.whole = bufs
        self.sems = sems
        self.one = rows // first.size
        self.two = self.got_two.shape[1]

    def rows(self, index, n, base=0):
        return pl.ds(pl.multiple_of(base + index * n, 16), n)

    def scatter_one(self):
        self.copies = []
        for n, who, index, _ in self.first.peers:
            src = self.local.at[self.rows(index, self.one, self.base)]
            self.copies.append(self.remote(src, self.got_one.at[n], self.sems[0].at[n], self.sems[1].at[n], who))
            self.copies[-1].start()

    def wait(self):
        for copy in self.copies:
            copy.wait()

    def scatter_two(self):
        self.wait()

        def tile(t, carry):
            start = pl.multiple_of(t * 16, 16)
            own = pl.ds(pl.multiple_of(self.base + self.first.me * self.one + start, 16), 16)
            total = self.local[own].astype(F32)
            for n, _, _, _ in self.first.peers:
                total = total + self.got_one[n, pl.ds(start, 16)].astype(F32)
            self.partial[pl.ds(start, 16)] = total.astype(BF)
            return carry

        lax.fori_loop(0, self.one // 16, tile, 0)
        spare = self.partial.shape[0] - self.one
        if spare:
            self.partial[self.one :] = jnp.zeros((spare, CH), BF)
        self.copies = []
        for n, who, index, _ in self.second.peers:
            src = self.partial.at[self.rows(index, self.two)]
            self.copies.append(self.remote(src, self.got_two.at[n], self.sems[2].at[n], self.sems[3].at[n], who))
            self.copies[-1].start()

    def gather_two(self, scale):
        self.wait()
        mine = self.rows(self.second.me, self.two)
        total = self.partial[mine].astype(F32)
        for n, _, _, _ in self.second.peers:
            total = total + self.got_two[n].astype(F32)
        self.whole[mine] = (total * scale).astype(BF)
        self.copies = []
        for n, who, _, _ in self.second.peers:
            block = self.whole.at[mine]
            self.copies.append(self.remote(block, block, self.sems[4].at[n], self.sems[5].at[n], who))
            self.copies[-1].start()

    def gather_one(self, core, partner):
        self.wait()
        home = self.rows(self.first.me, self.one, self.base)
        self.copies = []
        for n, who, _, _ in self.first.peers:
            src, dst = self.whole.at[: self.one], self.result.at[core, home]
            self.copies.append(self.remote(src, dst, self.sems[6].at[n], self.sems[7].at[n], who))
            self.copies[-1].start()
        self.result[core, home] = self.whole[: self.one]
        self.passed = []
        self.pass_on(core, partner, home, 0)

    def pass_on(self, core, partner, rows, n):
        block = self.result.at[core, rows]
        self.passed.append(self.remote(block, block, self.sems[8].at[n], self.sems[9].at[n], partner))
        self.passed[-1].start()

    def finish(self, core, partner, step):
        n, _, _, sender = self.first.peers[step]
        self.copies[step].wait()
        self.pass_on(core, partner, self.rows(sender, self.one, self.base), n)


class Group:
    def __init__(self, size, me, peers):
        self.size, self.me, self.peers = size, me, peers


class Halo:
    def __init__(self, refs):
        self.face, self.wall, self.edge, self.face_out, self.wall_out, self.diag_out, self.diag = refs


def kernel(dims, scale, *refs):
    (
        feat, occ, w1_hbm, bias, w2_hbm, cot, nbr, sx, sy,
        out_ref, gf_ref, gw_ref,
        w1, w2, mask, gate, fa0, fa1, fb0, fb1, za, zb, at, list_out, lists, gwo, gwm, crecv,
    ) = refs[:28]
    halos = [Halo(refs[28 + 7 * i : 35 + 7 * i]) for i in range(4)]
    bufs_q, bufs_p = refs[56:60], refs[60:64]
    w_sem, halo_s, halo_r, core_s, core_r = refs[64:69]
    sems_q, sems_p = refs[69:79], refs[79:89]
    nx, ny, nzhi, nzlo, _ = dims
    nz = nzhi * nzlo
    ngx, ngy = nzlo * ny * 2, nx * nzhi
    gx, gy = lax.axis_index("gx"), lax.axis_index("gy")
    core = lax.rem(gx, 2)
    y = lax.rem(gx // 2, ny)
    z = lax.rem(gy, nzhi) * nzlo + gx // (2 * ny)
    x = gy // nzhi

    def device(px, py, pz, c):
        return (lax.rem(pz, nzlo) * (2 * ny) + py * 2 + c, px * nzhi + pz // nzlo)

    near_x = [lax.rem(gx + 1, ngx), lax.rem(gx + ngx - 1, ngx)]
    near_y = [lax.rem(gy + 1, ngy), lax.rem(gy + ngy - 1, ngy)]
    partner = device(x, y, z, 1 - core)
    in_plane = []
    for i in range(nx):
        for k in range(ny):
            if i or k:
                px, py = lax.rem(x + i, nx), lax.rem(y + k, ny)
                back = lax.rem(x + nx - i, nx) * ny + lax.rem(y + ny - k, ny)
                in_plane.append((i * ny + k, device(px, py, z, core), px * ny + py, back))
    plane = Group(nx * ny, x * ny + y, in_plane)
    in_line = [
        (d, device(x, y, lax.rem(z + d, nz), core), lax.rem(z + d, nz), lax.rem(z + nz - d, nz))
        for d in range(1, nz)
    ]
    line = Group(nz, z, in_line)

    barrier = pltpu.get_barrier_semaphore()
    greet = [(px, gy) for px in near_x] + [(gx, py) for py in near_y]
    greet += [(px, py) for px in near_x for py in near_y]
    greet += [peer[1] for peer in in_plane + in_line]
    for who in greet:
        pl.semaphore_signal(barrier, inc=1, device_id=who, device_id_type=MESH)
    load_w1 = pltpu.make_async_copy(w1_hbm, w1, w_sem.at[0])
    load_w2 = pltpu.make_async_copy(w2_hbm, w2, w_sem.at[1])
    load_w1.start()
    load_w2.start()

    for t in range(4):
        halves = []
        for b in range(2):
            live = (nbr[b, 13] != NONE).astype(F32)
            row = occ[b : b + 1, t * CH : (t + 1) * CH].astype(F32) * live
            halves.append(jnp.broadcast_to(row, (CH, CH)).T.reshape(16, EDGE, CH))
        mask[t * 16 : (t + 1) * 16] = jnp.stack(halves, 1).reshape(16, 16, CH)

    def fields(p, carry):
        part = pl.ds(p * EDGE, EDGE)
        mk = mask[part]
        rows = pl.ds(pl.multiple_of(p * PLANE, PLANE), PLANE)
        for source, field in ((feat, fa0), (cot, fa1)):
            both = jnp.stack(
                [source[b, rows].astype(F32).reshape(EDGE, EDGE, CH) for b in range(2)], 1
            )
            field[part] = (both.reshape(EDGE, 16, CH) * mk).astype(BF)
        return carry

    lax.fori_loop(0, EDGE, fields, 0)

    def remote(src, dst, send, recv, who):
        return pltpu.make_async_remote_copy(
            src_ref=src, dst_ref=dst, send_sem=send, recv_sem=recv, device_id=who, device_id_type=MESH
        )

    def own_faces(field, halo):
        for side in range(2):
            halo.face[side, NONE] = jnp.zeros((PLANE, CH), BF)
            halo.wall[side, 6] = jnp.zeros((PLANE, CH), BF)
            halo.edge[side, NONE] = jnp.zeros((16, CH), BF)
            end = (1 - side) * (EDGE - 1)
            faces = field[end * EDGE : (end + 1) * EDGE].astype(F32).reshape(EDGE, 2, EDGE, CH)
            walls = jnp.stack([field[p * EDGE + end].astype(F32) for p in range(EDGE)], 0)
            walls = walls.reshape(EDGE, 2, EDGE, CH)
            face = [faces[:, b].reshape(PLANE, CH) for b in range(2)]
            wall = [walls[:, b].reshape(PLANE, CH) for b in range(2)]
            for b in range(2):
                halo.face[side, b] = face[b].astype(BF)
                halo.wall[side, b] = wall[b].astype(BF)
                ends = jnp.concatenate([face[b][:EDGE], face[b][PLANE - EDGE :]], 0)
                halo.edge[side, b] = ends.astype(BF)
            chosen = []
            for r in range(2):
                for listed, picks in ((sx, face), (sy, wall)):
                    slot = listed[side, r]
                    low = jnp.where(slot == 0, picks[0], 0.0)
                    chosen.append(jnp.where(slot == 1, picks[1], low))
            for r in range(2):
                halo.face_out[side, r] = chosen[2 * r].astype(BF)
                halo.wall_out[side, r] = chosen[2 * r + 1].astype(BF)
            tops = jnp.concatenate([chosen[2 * r + 1][PLANE - EDGE :] for r in range(2)], 0)
            bottoms = jnp.concatenate([chosen[2 * r + 1][:EDGE] for r in range(2)], 0)
            halo.diag_out[0, side] = tops.astype(BF)
            halo.diag_out[1, side] = bottoms.astype(BF)

    def halo_copies(n, halo):
        copies = []

        def add(src, dst, who):
            m = len(copies)
            copies.append(remote(src, dst, halo_s.at[n, m], halo_r.at[n, m], who))

        for d in range(2):
            add(halo.wall_out.at[d], halo.wall.at[d, 2 + 2 * d : 4 + 2 * d], (gx, near_y[d]))
        for d in range(2):
            for e in range(2):
                add(halo.diag_out.at[d, e], halo.diag.at[d, e], (near_x[d], near_y[e]))
        for d in range(2):
            add(halo.face_out.at[d], halo.face.at[d, 6 + 6 * d : 8 + 6 * d], (near_x[d], gy))
        if n == 0:
            for d in range(2):
                add(list_out.at[d], lists.at[d], (near_x[d], gy))
        return copies

    def far_edges(halo):
        blank = jnp.zeros((EDGE, CH), F32)
        for r in range(2, 6):
            got = halo.wall[(r - 2) // 2, r].astype(F32)
            for side, part in ((0, got[PLANE - EDGE :]), (1, got[:EDGE])):
                pair = [blank, part] if r < 4 else [part, blank]
                halo.edge[side, r] = jnp.concatenate(pair, 0).astype(BF)
        for side in range(2):
            below = halo.diag[side, 0].astype(F32)
            above = halo.diag[side, 1].astype(F32)
            table = lists[side].astype(F32)
            for r in range(6):
                row = jnp.broadcast_to(table[r : r + 1], (EDGE, CH))
                low, high = blank, blank
                if r < 2:
                    got = halo.face[side, 6 + 6 * side + r].astype(F32)
                    low, high = got[:EDGE], got[PLANE - EDGE :]
                for i in range(2):
                    part = slice(i * EDGE, (i + 1) * EDGE)
                    high = jnp.where(row == 2.0 + i, below[part], high)
                    low = jnp.where(row == 4.0 + i, above[part], low)
                halo.edge[side, 6 + 6 * side + r] = jnp.concatenate([low, high], 0).astype(BF)

    def inner(field, z_ref, f):
        linked = [[(nbr[b, 12 + 2 * d] != NONE).astype(F32) for b in range(2)] for d in range(2)]

        def layer(p, carry):
            own = field[pl.ds(p * EDGE, EDGE)].astype(F32).reshape(EDGE, 2, EDGE, CH)
            near = [jnp.stack([own[:, 1] * linked[d][0], own[:, 0] * linked[d][1]], 1) for d in range(2)]
            for e, rows in enumerate(with_z(own, *near)):
                z_ref[f, p + 1, 1 : EDGE + 1, :, e * CH : (e + 1) * CH] = rows
            return carry

        lax.fori_loop(0, EDGE, layer, 0)

    def shell(halo, z_ref, f):
        far_edges(halo)

        def three(first, load):
            pick = lambda k: jnp.stack([load(nbr[b, k]).astype(F32) for b in range(2)], 1)
            return pick(first + 1), pick(first), pick(first + 2)

        middle = slice(1, EDGE + 1)
        for side in range(2):
            end = (EDGE + 1) * side
            faces = three(18 * side + 3, lambda r: halo.face[side, r].reshape(EDGE, EDGE, CH))
            for e, rows in enumerate(with_z(*faces)):
                z_ref[f, end, middle, :, e * CH : (e + 1) * CH] = rows
            walls = three(
                9 + 6 * side, lambda r: halo.wall[side, jnp.minimum(r, 6)].reshape(EDGE, EDGE, CH)
            )
            for e, rows in enumerate(with_z(*walls)):
                z_ref[f, middle, end, :, e * CH : (e + 1) * CH] = rows
            for up in range(2):
                low = (1 - up) * EDGE
                lines = three(
                    18 * side + 6 * up,
                    lambda r: halo.edge[side, r].astype(F32)[low : low + EDGE].reshape(1, EDGE, CH),
                )
                for e, rows in enumerate(with_z(*lines)):
                    z_ref[f, end, (EDGE + 1) * up, :, e * CH : (e + 1) * CH] = rows[0]

    half = 2
    tiles = half * EDGE
    steps = EDGE // half
    taps = [(a, c) for a in range(3) for c in range(3)]

    def columns(z_ref, f, m):
        parts = [
            z_ref[f, pl.ds(m * half + a, half), c : c + EDGE].reshape(tiles * 16, 3 * CH) for a, c in taps
        ]
        return jnp.concatenate(parts, 1)

    def conv(z_ref, f, m, w):
        return jnp.dot(columns(z_ref, f, m), w[...], preferred_element_type=F32)

    def conv_t(z_ref, f, m, w):
        turned = jnp.concatenate([w[(KVOL - 1 - k) * CH : (KVOL - k) * CH] for k in range(KVOL)], 1)
        return lax.dot_general(
            columns(z_ref, f, m), turned, (((1,), (1,)), ((), ())), preferred_element_type=F32
        )

    for d in range(2):
        index = lax.broadcasted_iota(jnp.int32, (16, CH), 0)
        table = jnp.full((16, CH), float(NONE), F32)
        for r in range(6):
            table = jnp.where(index == r, sx[d, r].astype(F32), table)
        list_out[d] = table.astype(BF)
    own_faces(fa0, halos[0])
    own_faces(fa1, halos[1])
    copies = [halo_copies(n, halos[n]) for n in range(4)]
    pl.semaphore_wait(barrier, len(greet))
    for copy in copies[0] + copies[1]:
        copy.start()
    inner(fa0, za, 0)
    inner(fa1, za, 1)
    load_w1.wait()
    load_w2.wait()
    for copy in copies[0]:
        copy.wait()
    shell(halos[0], za, 0)

    def forward_layer(m, carry):
        part = pl.ds(m * tiles, tiles)
        mk = mask[part].reshape(tiles * 16, CH)
        preact = conv(za, 0, m, w1) + bias[...]
        hidden = (jnp.maximum(preact, 0.0) * mk).astype(BF)
        gate[part] = jnp.where(preact > 0, mk, 0.0).reshape(tiles, 16, CH)
        fb0[part] = hidden.reshape(tiles, 16, CH)
        at[1, m] = hidden.T
        return carry

    lax.fori_loop(0, steps, forward_layer, 0)
    own_faces(fb0, halos[2])
    for copy in copies[1]:
        copy.wait()
    for copy in copies[2]:
        copy.start()
    shell(halos[1], za, 1)

    def backward_layer(m, carry):
        part = pl.ds(m * tiles, tiles)
        grad = (conv_t(za, 1, m, w2) * gate[part].reshape(tiles * 16, CH)).astype(BF)
        fb1[part] = grad.reshape(tiles, 16, CH)
        at[0, m] = grad.T
        return carry

    lax.fori_loop(0, steps, backward_layer, 0)
    own_faces(fb1, halos[3])
    for copy in copies[3]:
        copy.start()

    third = 9 * CH

    def weight_grad(which, a, dst, add=None):
        left = jnp.concatenate([at[which, i] for i in range(steps)], 1)
        first = which == 0
        pa = jnp.where(first, a, 2 - a)
        for c in range(3):
            pc = jnp.where(first, c, 2 - c)
            right = za[which, pl.ds(pa, EDGE), pl.ds(pc, EDGE)].reshape(PLANE * 16, 3 * CH)
            prod = jnp.dot(left, right, preferred_element_type=F32)
            for e in range(3):
                plain = prod[:, (2 - e) * CH : (3 - e) * CH]
                turned = prod[:, e * CH : (e + 1) * CH].T
                block = jnp.where(first, turned, plain)
                row = (9 * a + 3 * c + e) * CH
                if add is not None:
                    block = block + add[row : row + CH].astype(F32)
                dst[row : row + CH] = block.astype(BF)

    core_copies = [
        remote(
            gwo.at[a * third : (a + 1) * third],
            crecv.at[a * third : (a + 1) * third],
            core_s.at[a],
            core_r.at[a],
            partner,
        )
        for a in range(3)
    ]
    for a in range(3):
        weight_grad(1 - core, a, gwo)
        core_copies[a].start()
    part_q = Part(remote, gwm, gw_ref, 0, third, line, plane, bufs_q, sems_q)
    part_p = Part(remote, gwm, gw_ref, third, 2 * third, plane, line, bufs_p, sems_p)
    for a in range(3):
        core_copies[a].wait()
        weight_grad(core, a, gwm, crecv)
        if a == 0:
            part_q.scatter_one()
    part_p.scatter_one()
    inner(fb0, zb, 0)
    inner(fb1, zb, 1)
    part_q.scatter_two()
    part_p.scatter_two()

    def write(value, dst, m):
        rows = pl.ds(pl.multiple_of(m * tiles * EDGE, tiles * EDGE), tiles * EDGE)
        bricks = value.reshape(tiles, 2, EDGE, CH)
        for b in range(2):
            dst[b, rows] = bricks[:, b].reshape(tiles * EDGE, CH).astype(BF)

    def second_layer(m, carry):
        part = pl.ds(m * tiles, tiles)
        masked = fa0[part].astype(F32).reshape(tiles * 16, CH)
        write(conv(zb, 0, m, w2) * mask[part].reshape(tiles * 16, CH) + masked, out_ref, m)
        return carry

    for copy in copies[2]:
        copy.wait()
    shell(halos[2], zb, 0)
    lax.fori_loop(0, steps, second_layer, 0)
    part_q.gather_two(scale)
    part_p.gather_two(scale)

    def last_layer(m, carry):
        part = pl.ds(m * tiles, tiles)
        given = fa1[part].astype(F32).reshape(tiles * 16, CH)
        write(conv_t(zb, 1, m, w1) * mask[part].reshape(tiles * 16, CH) + given, gf_ref, m)
        return carry

    for copy in copies[3]:
        copy.wait()
    shell(halos[3], zb, 1)
    lax.fori_loop(0, steps, last_layer, 0)
    part_q.gather_one(core, partner)
    part_p.gather_one(core, partner)
    for step in range(max(plane.size, line.size) - 1):
        for part in (part_q, part_p):
            if step < part.first.size - 1:
                part.finish(core, partner, step)
    for part in (part_q, part_p):
        for copy in part.passed:
            copy.wait()


def convert(out_in, gf_in, gw_in, out, gf, one, two):
    out[...] = out_in[...]
    gf[...] = gf_in[...]
    one[...] = gw_in[0].astype(F32)
    two[...] = gw_in[1].astype(F32)


def on_device(dims, features, occupied, weight_one, bias_one, weight_two, cotangent, neighbours, send_x, send_y):
    nx, ny, nzhi, nzlo, _ = dims
    nz, nxy = nzhi * nzlo, nx * ny
    slots, voxels, _ = features.shape
    scale = 1.0 / math.sqrt(slots * voxels * 2 * nxy * nz)
    vmem = pl.BlockSpec(memory_space=pltpu.VMEM)
    smem = pl.BlockSpec(memory_space=pltpu.SMEM)
    hbm = pl.BlockSpec(memory_space=pl.ANY)
    rows = KVOL * CH

    def halo():
        return [
            pltpu.VMEM((2, NONE + 1, PLANE, CH), BF),
            pltpu.VMEM((2, 7, PLANE, CH), BF),
            pltpu.VMEM((2, NONE + 1, 16, CH), BF),
            pltpu.VMEM((2, 2, PLANE, CH), BF),
            pltpu.VMEM((2, 2, PLANE, CH), BF),
            pltpu.VMEM((2, 2, 16, CH), BF),
            pltpu.VMEM((2, 2, 16, CH), BF),
        ]

    sem = lambda *shape: pltpu.SemaphoreType.DMA(shape)

    def part(total, n_one, n_two):
        one = total // n_one
        two = -(-one // (16 * n_two)) * 16
        bufs = [
            pltpu.VMEM((n_one, one, CH), BF),
            pltpu.VMEM((n_two * two, CH), BF),
            pltpu.VMEM((n_two, two, CH), BF),
            pltpu.VMEM((n_two * two, CH), BF),
        ]
        sizes = (n_one, n_one, n_two, n_two, n_two, n_two, n_one, n_one, n_one, n_one)
        return bufs, [sem(n) for n in sizes]

    bufs_q, sems_q = part(rows // 3, nz, nxy)
    bufs_p, sems_p = part(2 * rows // 3, nxy, nz)
    field = pltpu.VMEM((PLANE, 16, CH), BF)
    weight = pltpu.VMEM((rows, CH), BF)
    plain = pltpu.VMEM((PLANE, 16, CH), F32)
    padded = pltpu.VMEM((2, EDGE + 2, EDGE + 2, 16, 3 * CH), BF)
    lists = pltpu.VMEM((2, 16, CH), BF)
    made = pl.pallas_call(
        functools.partial(kernel, dims, scale),
        out_shape=(
            jax.ShapeDtypeStruct(features.shape, BF),
            jax.ShapeDtypeStruct(features.shape, BF),
            jax.ShapeDtypeStruct((2, rows, CH), BF),
        ),
        in_specs=[vmem, vmem, hbm, vmem, hbm, vmem, smem, smem, smem],
        out_specs=(vmem, vmem, vmem),
        scratch_shapes=[
            weight, weight, plain, plain, field, field, field, field, padded, padded,
            pltpu.VMEM((2, 4, CH, 256), BF),
            lists, lists, weight, weight, weight,
            *halo(), *halo(), *halo(), *halo(),
            *bufs_q, *bufs_p,
            sem(2), sem(4, 10), sem(4, 10), sem(3), sem(3),
            *sems_q, *sems_p,
        ],
        compiler_params=pltpu.CompilerParams(
            collective_id=0, has_side_effects=True, vmem_limit_bytes=56 * 2**20
        ),
    )(
        features,
        occupied,
        weight_one.reshape(rows, CH),
        bias_one.reshape(1, CH),
        weight_two.reshape(rows, CH),
        cotangent,
        neighbours,
        send_x.reshape(2, -1),
        send_y.reshape(2, -1),
    )
    cuts = 4
    brick = pl.BlockSpec((slots, voxels // cuts, CH), lambda i: (0, i, 0))
    grad = pl.BlockSpec((rows // cuts, CH), lambda i: (i, 0))
    out, grad_features, one, two = pl.pallas_call(
        convert,
        grid=(cuts,),
        out_shape=(
            jax.ShapeDtypeStruct(features.shape, BF),
            jax.ShapeDtypeStruct(features.shape, BF),
            jax.ShapeDtypeStruct((rows, CH), F32),
            jax.ShapeDtypeStruct((rows, CH), F32),
        ),
        in_specs=[brick, brick, pl.BlockSpec((2, rows // cuts, CH), lambda i: (0, i, 0))],
        out_specs=(brick, brick, grad, grad),
        compiler_params=pltpu.CompilerParams(vmem_limit_bytes=24 * 2**20),
    )(*made)
    return (out, grad_features, one.reshape(KVOL, CH, CH), two.reshape(KVOL, CH, CH))


def solution(mesh, dims=SLICE):
    in_specs = (
        P(("gx", "gy"), None, None),
        P(("gx", "gy"), None),
        P(),
        P(),
        P(),
        P(("gx", "gy"), None, None),
        P(("gx", "gy"), None),
        P(("gx", "gy"), None, None),
        P(("gx", "gy"), None, None),
    )
    out_specs = (P(("gx", "gy"), None, None), P(("gx", "gy"), None, None), P(), P())
    return jax.shard_map(
        functools.partial(on_device, dims), mesh=mesh, in_specs=in_specs, out_specs=out_specs, check_vma=False
    )
```

```python
import functools
import math

import jax
import jax.numpy as jnp
from jax import lax
from jax.experimental import pallas as pl
from jax.experimental.pallas import tpu as pltpu
from jax.sharding import PartitionSpec as P

EDGE = 8
KVOL = 27
CH = 128
PLANE = EDGE * EDGE
NONE = 18
BF = jnp.bfloat16
F32 = jnp.float32
MESH = pl.DeviceIdType.MESH
SLICE = (4, 4, 2, 4, 2)


def with_z(line, below, above):
    n = line.shape[0]
    flat = lambda t: t.reshape(n * 2, EDGE, CH)
    line, below, above = flat(line), flat(below), flat(above)
    level = lax.broadcasted_iota(jnp.int32, line.shape, 1)
    down = pltpu.roll(jnp.where(level == EDGE - 1, below, line), 1, 1)
    up = pltpu.roll(jnp.where(level == 0, above, line), EDGE - 1, 1)
    return [t.reshape(n, 2 * EDGE, CH).astype(BF) for t in (down, line, up)]


class Part:
    def __init__(self, remote, local, result, base, rows, first, second, bufs, sems):
        self.remote, self.local, self.result = remote, local, result
        self.base, self.first, self.second = base, first, second
        self.got_one, self.partial, self.got_two, self.whole = bufs
        self.sems = sems
        self.one = rows // first.size
        self.two = self.got_two.shape[1]

    def rows(self, index, n, base=0):
        return pl.ds(pl.multiple_of(base + index * n, 16), n)

    def scatter_one(self):
        self.copies = []
        for n, who, index, _ in self.first.peers:
            src = self.local.at[self.rows(index, self.one, self.base)]
            self.copies.append(self.remote(src, self.got_one.at[n], self.sems[0].at[n], self.sems[1].at[n], who))
            self.copies[-1].start()

    def wait(self):
        for copy in self.copies:
            copy.wait()

    def scatter_two(self):
        self.wait()

        def tile(t, carry):
            start = pl.multiple_of(t * 16, 16)
            own = pl.ds(pl.multiple_of(self.base + self.first.me * self.one + start, 16), 16)
            total = self.local[own].astype(F32)
            for n, _, _, _ in self.first.peers:
                total = total + self.got_one[n, pl.ds(start, 16)].astype(F32)
            self.partial[pl.ds(start, 16)] = total.astype(BF)
            return carry

        lax.fori_loop(0, self.one // 16, tile, 0)
        spare = self.partial.shape[0] - self.one
        if spare:
            self.partial[self.one :] = jnp.zeros((spare, CH), BF)
        self.copies = []
        for n, who, index, _ in self.second.peers:
            src = self.partial.at[self.rows(index, self.two)]
            self.copies.append(self.remote(src, self.got_two.at[n], self.sems[2].at[n], self.sems[3].at[n], who))
            self.copies[-1].start()

    def gather_two(self, scale):
        self.wait()
        mine = self.rows(self.second.me, self.two)
        total = self.partial[mine].astype(F32)
        for n, _, _, _ in self.second.peers:
            total = total + self.got_two[n].astype(F32)
        self.whole[mine] = (total * scale).astype(BF)
        self.copies = []
        for n, who, _, _ in self.second.peers:
            block = self.whole.at[mine]
            self.copies.append(self.remote(block, block, self.sems[4].at[n], self.sems[5].at[n], who))
            self.copies[-1].start()

    def gather_one(self, core, partner):
        self.wait()
        home = self.rows(self.first.me, self.one, self.base)
        self.copies = []
        for n, who, _, _ in self.first.peers:
            src, dst = self.whole.at[: self.one], self.result.at[core, home]
            self.copies.append(self.remote(src, dst, self.sems[6].at[n], self.sems[7].at[n], who))
            self.copies[-1].start()
        self.result[core, home] = self.whole[: self.one]
        self.passed = []
        self.pass_on(core, partner, home, 0)

    def pass_on(self, core, partner, rows, n):
        block = self.result.at[core, rows]
        self.passed.append(self.remote(block, block, self.sems[8].at[n], self.sems[9].at[n], partner))
        self.passed[-1].start()

    def finish(self, core, partner, step):
        n, _, _, sender = self.first.peers[step]
        self.copies[step].wait()
        self.pass_on(core, partner, self.rows(sender, self.one, self.base), n)


class Group:
    def __init__(self, size, me, peers):
        self.size, self.me, self.peers = size, me, peers


class Halo:
    def __init__(self, refs):
        self.face, self.wall, self.edge, self.face_out, self.wall_out, self.diag_out, self.diag = refs


def kernel(dims, scale, *refs):
    (
        feat, occ, w1_hbm, bias, w2_hbm, cot, nbr, sx, sy,
        out_ref, gf_ref, gw_ref,
        w1, w2, mask, gate, sum0, sum1, fa0, fa1, fb0, fb1, za, zb, at, list_out, lists, gwo, gwm, crecv,
    ) = refs[:30]
    refs = refs[2:]
    halos = [Halo(refs[28 + 7 * i : 35 + 7 * i]) for i in range(4)]
    bufs_q, bufs_p = refs[56:60], refs[60:64]
    w_sem, halo_s, halo_r, core_s, core_r = refs[64:69]
    sems_q, sems_p = refs[69:79], refs[79:89]
    nx, ny, nzhi, nzlo, _ = dims
    nz = nzhi * nzlo
    ngx, ngy = nzlo * ny * 2, nx * nzhi
    gx, gy = lax.axis_index("gx"), lax.axis_index("gy")
    core = lax.rem(gx, 2)
    y = lax.rem(gx // 2, ny)
    z = lax.rem(gy, nzhi) * nzlo + gx // (2 * ny)
    x = gy // nzhi

    def device(px, py, pz, c):
        return (lax.rem(pz, nzlo) * (2 * ny) + py * 2 + c, px * nzhi + pz // nzlo)

    near_x = [lax.rem(gx + 1, ngx), lax.rem(gx + ngx - 1, ngx)]
    near_y = [lax.rem(gy + 1, ngy), lax.rem(gy + ngy - 1, ngy)]
    partner = device(x, y, z, 1 - core)
    in_plane = []
    for i in range(nx):
        for k in range(ny):
            if i or k:
                px, py = lax.rem(x + i, nx), lax.rem(y + k, ny)
                back = lax.rem(x + nx - i, nx) * ny + lax.rem(y + ny - k, ny)
                in_plane.append((i * ny + k, device(px, py, z, core), px * ny + py, back))
    plane = Group(nx * ny, x * ny + y, in_plane)
    in_line = [
        (d, device(x, y, lax.rem(z + d, nz), core), lax.rem(z + d, nz), lax.rem(z + nz - d, nz))
        for d in range(1, nz)
    ]
    line = Group(nz, z, in_line)

    barrier = pltpu.get_barrier_semaphore()
    greet = [(px, gy) for px in near_x] + [(gx, py) for py in near_y]
    greet += [(px, py) for px in near_x for py in near_y]
    greet += [peer[1] for peer in in_plane + in_line]
    for who in greet:
        pl.semaphore_signal(barrier, inc=1, device_id=who, device_id_type=MESH)
    load_w1 = pltpu.make_async_copy(w1_hbm, w1, w_sem.at[0])
    load_w2 = pltpu.make_async_copy(w2_hbm, w2, w_sem.at[1])
    load_w1.start()
    load_w2.start()

    for t in range(4):
        halves = []
        for b in range(2):
            live = (nbr[b, 13] != NONE).astype(F32)
            row = occ[b : b + 1, t * CH : (t + 1) * CH].astype(F32) * live
            halves.append(jnp.broadcast_to(row, (CH, CH)).T.reshape(16, EDGE, CH))
        mask[t * 16 : (t + 1) * 16] = jnp.stack(halves, 1).reshape(16, 16, CH)

    def masked_field(source, field):
        def layer(p, carry):
            part = pl.ds(p * EDGE, EDGE)
            rows = pl.ds(pl.multiple_of(p * PLANE, PLANE), PLANE)
            both = jnp.stack(
                [source[b, rows].astype(F32).reshape(EDGE, EDGE, CH) for b in range(2)], 1
            )
            field[part] = (both.reshape(EDGE, 16, CH) * mask[part]).astype(BF)
            return carry

        lax.fori_loop(0, EDGE, layer, 0)

    def remote(src, dst, send, recv, who):
        return pltpu.make_async_remote_copy(
            src_ref=src, dst_ref=dst, send_sem=send, recv_sem=recv, device_id=who, device_id_type=MESH
        )

    def own_faces(field, halo):
        for side in range(2):
            halo.face[side, NONE] = jnp.zeros((PLANE, CH), BF)
            halo.wall[side, 6] = jnp.zeros((PLANE, CH), BF)
            halo.edge[side, NONE] = jnp.zeros((16, CH), BF)
            end = (1 - side) * (EDGE - 1)
            faces = field[end * EDGE : (end + 1) * EDGE].astype(F32).reshape(EDGE, 2, EDGE, CH)
            walls = jnp.stack([field[p * EDGE + end].astype(F32) for p in range(EDGE)], 0)
            walls = walls.reshape(EDGE, 2, EDGE, CH)
            face = [faces[:, b].reshape(PLANE, CH) for b in range(2)]
            wall = [walls[:, b].reshape(PLANE, CH) for b in range(2)]
            for b in range(2):
                halo.face[side, b] = face[b].astype(BF)
                halo.wall[side, b] = wall[b].astype(BF)
                ends = jnp.concatenate([face[b][:EDGE], face[b][PLANE - EDGE :]], 0)
                halo.edge[side, b] = ends.astype(BF)
            chosen = []
            for r in range(2):
                for listed, picks in ((sx, face), (sy, wall)):
                    slot = listed[side, r]
                    low = jnp.where(slot == 0, picks[0], 0.0)
                    chosen.append(jnp.where(slot == 1, picks[1], low))
            for r in range(2):
                halo.face_out[side, r] = chosen[2 * r].astype(BF)
                halo.wall_out[side, r] = chosen[2 * r + 1].astype(BF)
            tops = jnp.concatenate([chosen[2 * r + 1][PLANE - EDGE :] for r in range(2)], 0)
            bottoms = jnp.concatenate([chosen[2 * r + 1][:EDGE] for r in range(2)], 0)
            halo.diag_out[0, side] = tops.astype(BF)
            halo.diag_out[1, side] = bottoms.astype(BF)

    def halo_copies(n, halo):
        copies = []

        def add(src, dst, who):
            m = len(copies)
            copies.append(remote(src, dst, halo_s.at[n, m], halo_r.at[n, m], who))

        for d in range(2):
            add(halo.wall_out.at[d], halo.wall.at[d, 2 + 2 * d : 4 + 2 * d], (gx, near_y[d]))
        for d in range(2):
            for e in range(2):
                add(halo.diag_out.at[d, e], halo.diag.at[d, e], (near_x[d], near_y[e]))
        for d in range(2):
            add(halo.face_out.at[d], halo.face.at[d, 6 + 6 * d : 8 + 6 * d], (near_x[d], gy))
        if n == 0:
            for d in range(2):
                add(list_out.at[d], lists.at[d], (near_x[d], gy))
        return copies

    def far_edges(halo):
        blank = jnp.zeros((EDGE, CH), F32)
        for r in range(2, 6):
            got = halo.wall[(r - 2) // 2, r].astype(F32)
            for side, part in ((0, got[PLANE - EDGE :]), (1, got[:EDGE])):
                pair = [blank, part] if r < 4 else [part, blank]
                halo.edge[side, r] = jnp.concatenate(pair, 0).astype(BF)
        for side in range(2):
            below = halo.diag[side, 0].astype(F32)
            above = halo.diag[side, 1].astype(F32)
            table = lists[side].astype(F32)
            for r in range(6):
                row = jnp.broadcast_to(table[r : r + 1], (EDGE, CH))
                low, high = blank, blank
                if r < 2:
                    got = halo.face[side, 6 + 6 * side + r].astype(F32)
                    low, high = got[:EDGE], got[PLANE - EDGE :]
                for i in range(2):
                    part = slice(i * EDGE, (i + 1) * EDGE)
                    high = jnp.where(row == 2.0 + i, below[part], high)
                    low = jnp.where(row == 4.0 + i, above[part], low)
                halo.edge[side, 6 + 6 * side + r] = jnp.concatenate([low, high], 0).astype(BF)

    def inner(field, z_ref, f):
        linked = [[(nbr[b, 12 + 2 * d] != NONE).astype(F32) for b in range(2)] for d in range(2)]

        def layer(p, carry):
            own = field[pl.ds(p * EDGE, EDGE)].astype(F32).reshape(EDGE, 2, EDGE, CH)
            near = [jnp.stack([own[:, 1] * linked[d][0], own[:, 0] * linked[d][1]], 1) for d in range(2)]
            for e, rows in enumerate(with_z(own, *near)):
                z_ref[f, p + 1, 1 : EDGE + 1, :, e * CH : (e + 1) * CH] = rows
            return carry

        lax.fori_loop(0, EDGE, layer, 0)

    def shell(halo, z_ref, f):
        far_edges(halo)

        def three(first, load):
            pick = lambda k: jnp.stack([load(nbr[b, k]).astype(F32) for b in range(2)], 1)
            return pick(first + 1), pick(first), pick(first + 2)

        middle = slice(1, EDGE + 1)
        for side in range(2):
            end = (EDGE + 1) * side
            faces = three(18 * side + 3, lambda r: halo.face[side, r].reshape(EDGE, EDGE, CH))
            for e, rows in enumerate(with_z(*faces)):
                z_ref[f, end, middle, :, e * CH : (e + 1) * CH] = rows
            walls = three(
                9 + 6 * side, lambda r: halo.wall[side, jnp.minimum(r, 6)].reshape(EDGE, EDGE, CH)
            )
            for e, rows in enumerate(with_z(*walls)):
                z_ref[f, middle, end, :, e * CH : (e + 1) * CH] = rows
            for up in range(2):
                low = (1 - up) * EDGE
                lines = three(
                    18 * side + 6 * up,
                    lambda r: halo.edge[side, r].astype(F32)[low : low + EDGE].reshape(1, EDGE, CH),
                )
                for e, rows in enumerate(with_z(*lines)):
                    z_ref[f, end, (EDGE + 1) * up, :, e * CH : (e + 1) * CH] = rows[0]

    half = 2
    tiles = half * EDGE
    steps = EDGE // half
    taps = [(a, c) for a in range(3) for c in range(3)]

    def columns(z_ref, f, m):
        parts = [
            z_ref[f, pl.ds(m * half + a, half), c : c + EDGE].reshape(tiles * 16, 3 * CH) for a, c in taps
        ]
        return jnp.concatenate(parts, 1)

    def conv(z_ref, f, m, w):
        return jnp.dot(columns(z_ref, f, m), w[...], preferred_element_type=F32)

    def conv_t(z_ref, f, m, w):
        turned = jnp.concatenate([w[(KVOL - 1 - k) * CH : (KVOL - k) * CH] for k in range(KVOL)], 1)
        return lax.dot_general(
            columns(z_ref, f, m), turned, (((1,), (1,)), ((), ())), preferred_element_type=F32
        )

    for d in range(2):
        index = lax.broadcasted_iota(jnp.int32, (16, CH), 0)
        table = jnp.full((16, CH), float(NONE), F32)
        for r in range(6):
            table = jnp.where(index == r, sx[d, r].astype(F32), table)
        list_out[d] = table.astype(BF)
    masked_field(feat, fa0)
    own_faces(fa0, halos[0])
    copies = [halo_copies(n, halos[n]) for n in range(4)]
    pl.semaphore_wait(barrier, len(greet))
    for copy in copies[0]:
        copy.start()
    masked_field(cot, fa1)
    own_faces(fa1, halos[1])
    for copy in copies[1]:
        copy.start()

    for f in range(2):
        for end in (0, EDGE + 1):
            za[f, end] = jnp.zeros((EDGE + 2, 16, 3 * CH), BF)
            za[f, 1 : EDGE + 1, end] = jnp.zeros((EDGE, 16, 3 * CH), BF)
    inner(fa0, za, 0)
    load_w1.wait()

    def inside_forward(m, carry):
        sum0[pl.ds(m * tiles, tiles)] = conv(za, 0, m, w1).reshape(tiles, 16, CH)
        return carry

    lax.fori_loop(0, steps, inside_forward, 0)
    inner(fa1, za, 1)
    load_w2.wait()

    def inside_backward(m, carry):
        sum1[pl.ds(m * tiles, tiles)] = conv_t(za, 1, m, w2).reshape(tiles, 16, CH)
        return carry

    lax.fori_loop(0, steps, inside_backward, 0)

    def sides(f, w, total, turned):
        def times(parts, which):
            left = jnp.concatenate([t.reshape(EDGE * 16, 3 * CH) for t in parts], 1)
            if turned:
                blocks = [
                    w[(KVOL - 1 - k) * CH : (KVOL - k) * CH]
                    for a, c in which
                    for k in range(9 * a + 3 * c, 9 * a + 3 * c + 3)
                ]
                right = jnp.concatenate(blocks, 1)
                got = lax.dot_general(left, right, (((1,), (1,)), ((), ())), preferred_element_type=F32)
            else:
                right = jnp.concatenate([w[(3 * a + c) * 3 * CH : (3 * a + c + 1) * 3 * CH] for a, c in which], 0)
                got = jnp.dot(left, right, preferred_element_type=F32)
            return got.reshape(EDGE, 16, CH)

        none = jnp.zeros((1, 16, 3 * CH), BF)
        for side in range(2):
            shell_at, inner_at, tap = (EDGE + 1) * side, (EDGE - 1) * side, 2 * side
            parts = [za[f, shell_at, c : c + EDGE] for c in range(3)]
            rows = slice(inner_at * EDGE, (inner_at + 1) * EDGE)
            total[rows] = total[rows] + times(parts, [(tap, c) for c in range(3)])
            wall = za[f, 1 : EDGE + 1, shell_at]
            parts = [
                jnp.concatenate([none, wall[: EDGE - 1]], 0),
                wall,
                jnp.concatenate([wall[1:], none], 0),
            ]
            more = times(parts, [(a, tap) for a in range(3)])
            for p in range(EDGE):
                total[p * EDGE + inner_at] = total[p * EDGE + inner_at] + more[p]

    for copy in copies[0]:
        copy.wait()
    shell(halos[0], za, 0)
    sides(0, w1, sum0, False)

    def forward_layer(m, carry):
        part = pl.ds(m * tiles, tiles)
        mk = mask[part].reshape(tiles * 16, CH)
        preact = sum0[part].reshape(tiles * 16, CH) + bias[...]
        hidden = (jnp.maximum(preact, 0.0) * mk).astype(BF)
        gate[part] = jnp.where(preact > 0, mk, 0.0).reshape(tiles, 16, CH)
        fb0[part] = hidden.reshape(tiles, 16, CH)
        at[1, m] = hidden.T
        return carry

    lax.fori_loop(0, steps, forward_layer, 0)
    for copy in copies[1]:
        copy.wait()
    shell(halos[1], za, 1)
    sides(1, w2, sum1, True)

    def backward_layer(m, carry):
        part = pl.ds(m * tiles, tiles)
        grad = (sum1[part] * gate[part]).reshape(tiles * 16, CH).astype(BF)
        fb1[part] = grad.reshape(tiles, 16, CH)
        at[0, m] = grad.T
        return carry

    lax.fori_loop(0, steps, backward_layer, 0)

    third = 9 * CH

    def weight_grad(which, a, dst, add=None):
        left = jnp.concatenate([at[which, i] for i in range(steps)], 1)
        first = which == 0
        pa = jnp.where(first, a, 2 - a)
        for c in range(3):
            pc = jnp.where(first, c, 2 - c)
            right = za[which, pl.ds(pa, EDGE), pl.ds(pc, EDGE)].reshape(PLANE * 16, 3 * CH)
            prod = jnp.dot(left, right, preferred_element_type=F32)
            for e in range(3):
                plain = prod[:, (2 - e) * CH : (3 - e) * CH]
                turned = prod[:, e * CH : (e + 1) * CH].T
                block = jnp.where(first, turned, plain)
                row = (9 * a + 3 * c + e) * CH
                if add is not None:
                    block = block + add[row : row + CH].astype(F32)
                dst[row : row + CH] = block.astype(BF)

    core_copies = [
        remote(
            gwo.at[a * third : (a + 1) * third],
            crecv.at[a * third : (a + 1) * third],
            core_s.at[a],
            core_r.at[a],
            partner,
        )
        for a in range(3)
    ]
    for a in range(3):
        weight_grad(1 - core, a, gwo)
        core_copies[a].start()
    part_q = Part(remote, gwm, gw_ref, 0, third, line, plane, bufs_q, sems_q)
    part_p = Part(remote, gwm, gw_ref, third, 2 * third, plane, line, bufs_p, sems_p)
    for a in range(3):
        core_copies[a].wait()
        weight_grad(core, a, gwm, crecv)
        if a == 0:
            part_q.scatter_one()
    part_p.scatter_one()
    own_faces(fb0, halos[2])
    for copy in copies[2]:
        copy.start()
    own_faces(fb1, halos[3])
    for copy in copies[3]:
        copy.start()
    inner(fb0, zb, 0)
    inner(fb1, zb, 1)
    part_q.scatter_two()
    part_p.scatter_two()

    def write(value, dst, m):
        rows = pl.ds(pl.multiple_of(m * tiles * EDGE, tiles * EDGE), tiles * EDGE)
        bricks = value.reshape(tiles, 2, EDGE, CH)
        for b in range(2):
            dst[b, rows] = bricks[:, b].reshape(tiles * EDGE, CH).astype(BF)

    def second_layer(m, carry):
        part = pl.ds(m * tiles, tiles)
        masked = fa0[part].astype(F32).reshape(tiles * 16, CH)
        write(conv(zb, 0, m, w2) * mask[part].reshape(tiles * 16, CH) + masked, out_ref, m)
        return carry

    for copy in copies[2]:
        copy.wait()
    shell(halos[2], zb, 0)
    lax.fori_loop(0, steps, second_layer, 0)
    part_q.gather_two(scale)
    part_p.gather_two(scale)

    def last_layer(m, carry):
        part = pl.ds(m * tiles, tiles)
        given = fa1[part].astype(F32).reshape(tiles * 16, CH)
        write(conv_t(zb, 1, m, w1) * mask[part].reshape(tiles * 16, CH) + given, gf_ref, m)
        return carry

    for copy in copies[3]:
        copy.wait()
    shell(halos[3], zb, 1)
    lax.fori_loop(0, steps, last_layer, 0)
    part_q.gather_one(core, partner)
    part_p.gather_one(core, partner)
    for step in range(max(plane.size, line.size) - 1):
        for part in (part_q, part_p):
            if step < part.first.size - 1:
                part.finish(core, partner, step)
    for part in (part_q, part_p):
        for copy in part.passed:
            copy.wait()


def convert(out_in, gf_in, gw_in, out, gf, one, two):
    out[...] = out_in[...]
    gf[...] = gf_in[...]
    one[...] = gw_in[0].astype(F32)
    two[...] = gw_in[1].astype(F32)


def on_device(dims, features, occupied, weight_one, bias_one, weight_two, cotangent, neighbours, send_x, send_y):
    nx, ny, nzhi, nzlo, _ = dims
    nz, nxy = nzhi * nzlo, nx * ny
    slots, voxels, _ = features.shape
    scale = 1.0 / math.sqrt(slots * voxels * 2 * nxy * nz)
    vmem = pl.BlockSpec(memory_space=pltpu.VMEM)
    smem = pl.BlockSpec(memory_space=pltpu.SMEM)
    hbm = pl.BlockSpec(memory_space=pl.ANY)
    rows = KVOL * CH

    def halo():
        return [
            pltpu.VMEM((2, NONE + 1, PLANE, CH), BF),
            pltpu.VMEM((2, 7, PLANE, CH), BF),
            pltpu.VMEM((2, NONE + 1, 16, CH), BF),
            pltpu.VMEM((2, 2, PLANE, CH), BF),
            pltpu.VMEM((2, 2, PLANE, CH), BF),
            pltpu.VMEM((2, 2, 16, CH), BF),
            pltpu.VMEM((2, 2, 16, CH), BF),
        ]

    sem = lambda *shape: pltpu.SemaphoreType.DMA(shape)

    def part(total, n_one, n_two):
        one = total // n_one
        two = -(-one // (16 * n_two)) * 16
        bufs = [
            pltpu.VMEM((n_one, one, CH), BF),
            pltpu.VMEM((n_two * two, CH), BF),
            pltpu.VMEM((n_two, two, CH), BF),
            pltpu.VMEM((n_two * two, CH), BF),
        ]
        sizes = (n_one, n_one, n_two, n_two, n_two, n_two, n_one, n_one, n_one, n_one)
        return bufs, [sem(n) for n in sizes]

    bufs_q, sems_q = part(rows // 3, nz, nxy)
    bufs_p, sems_p = part(2 * rows // 3, nxy, nz)
    field = pltpu.VMEM((PLANE, 16, CH), BF)
    weight = pltpu.VMEM((rows, CH), BF)
    plain = pltpu.VMEM((PLANE, 16, CH), F32)
    padded = pltpu.VMEM((2, EDGE + 2, EDGE + 2, 16, 3 * CH), BF)
    lists = pltpu.VMEM((2, 16, CH), BF)
    made = pl.pallas_call(
        functools.partial(kernel, dims, scale),
        out_shape=(
            jax.ShapeDtypeStruct(features.shape, BF),
            jax.ShapeDtypeStruct(features.shape, BF),
            jax.ShapeDtypeStruct((2, rows, CH), BF),
        ),
        in_specs=[vmem, vmem, hbm, vmem, hbm, vmem, smem, smem, smem],
        out_specs=(vmem, vmem, vmem),
        scratch_shapes=[
            weight, weight, plain, plain, plain, plain, field, field, field, field, padded, padded,
            pltpu.VMEM((2, 4, CH, 256), BF),
            lists, lists, weight, weight, weight,
            *halo(), *halo(), *halo(), *halo(),
            *bufs_q, *bufs_p,
            sem(2), sem(4, 10), sem(4, 10), sem(3), sem(3),
            *sems_q, *sems_p,
        ],
        compiler_params=pltpu.CompilerParams(
            collective_id=0, has_side_effects=True, vmem_limit_bytes=56 * 2**20
        ),
    )(
        features,
        occupied,
        weight_one.reshape(rows, CH),
        bias_one.reshape(1, CH),
        weight_two.reshape(rows, CH),
        cotangent,
        neighbours,
        send_x.reshape(2, -1),
        send_y.reshape(2, -1),
    )
    cuts = 4
    brick = pl.BlockSpec((slots, voxels // cuts, CH), lambda i: (0, i, 0))
    grad = pl.BlockSpec((rows // cuts, CH), lambda i: (i, 0))
    out, grad_features, one, two = pl.pallas_call(
        convert,
        grid=(cuts,),
        out_shape=(
            jax.ShapeDtypeStruct(features.shape, BF),
            jax.ShapeDtypeStruct(features.shape, BF),
            jax.ShapeDtypeStruct((rows, CH), F32),
            jax.ShapeDtypeStruct((rows, CH), F32),
        ),
        in_specs=[brick, brick, pl.BlockSpec((2, rows // cuts, CH), lambda i: (0, i, 0))],
        out_specs=(brick, brick, grad, grad),
        compiler_params=pltpu.CompilerParams(vmem_limit_bytes=60 * 2**20),
    )(*made)
    return (out, grad_features, one.reshape(KVOL, CH, CH), two.reshape(KVOL, CH, CH))


def solution(mesh, dims=SLICE):
    in_specs = (
        P(("gx", "gy"), None, None),
        P(("gx", "gy"), None),
        P(),
        P(),
        P(),
        P(("gx", "gy"), None, None),
        P(("gx", "gy"), None),
        P(("gx", "gy"), None, None),
        P(("gx", "gy"), None, None),
    )
    out_specs = (P(("gx", "gy"), None, None), P(("gx", "gy"), None, None), P(), P())
    return jax.shard_map(
        functools.partial(on_device, dims), mesh=mesh, in_specs=in_specs, out_specs=out_specs, check_vma=False
    )
```

```python
import functools
import math

import jax
import jax.numpy as jnp
from jax import lax
from jax.experimental import pallas as pl
from jax.experimental.pallas import tpu as pltpu
from jax.sharding import PartitionSpec as P

EDGE = 8
KVOL = 27
CH = 128
PLANE = EDGE * EDGE
NONE = 18
BF = jnp.bfloat16
F32 = jnp.float32
MESH = pl.DeviceIdType.MESH
SLICE = (4, 4, 2, 4, 2)


def with_z(line, below, above):
    n = line.shape[0]
    flat = lambda t: t.reshape(n * 2, EDGE, CH)
    line, below, above = flat(line), flat(below), flat(above)
    level = lax.broadcasted_iota(jnp.int32, line.shape, 1)
    down = pltpu.roll(jnp.where(level == EDGE - 1, below, line), 1, 1)
    up = pltpu.roll(jnp.where(level == 0, above, line), EDGE - 1, 1)
    return [t.reshape(n, 2 * EDGE, CH).astype(BF) for t in (down, line, up)]


class Part:
    def __init__(self, remote, local, result, base, rows, first, second, bufs, sems):
        self.remote, self.local, self.result = remote, local, result
        self.base, self.first, self.second = base, first, second
        self.got_one, self.partial, self.got_two, self.whole = bufs
        self.sems = sems
        self.one = rows // first.size
        self.two = self.got_two.shape[1]

    def rows(self, index, n, base=0):
        return pl.ds(pl.multiple_of(base + index * n, 16), n)

    def scatter_one(self):
        self.copies = []
        for n, who, index, _ in self.first.peers:
            src = self.local.at[self.rows(index, self.one, self.base)]
            self.copies.append(self.remote(src, self.got_one.at[n], self.sems[0].at[n], self.sems[1].at[n], who))
            self.copies[-1].start()

    def wait(self):
        for copy in self.copies:
            copy.wait()

    def scatter_two(self):
        self.wait()

        def tile(t, carry):
            start = pl.multiple_of(t * 16, 16)
            own = pl.ds(pl.multiple_of(self.base + self.first.me * self.one + start, 16), 16)
            total = self.local[own].astype(F32)
            for n, _, _, _ in self.first.peers:
                total = total + self.got_one[n, pl.ds(start, 16)].astype(F32)
            self.partial[pl.ds(start, 16)] = total.astype(BF)
            return carry

        lax.fori_loop(0, self.one // 16, tile, 0)
        spare = self.partial.shape[0] - self.one
        if spare:
            self.partial[self.one :] = jnp.zeros((spare, CH), BF)
        self.copies = []
        for n, who, index, _ in self.second.peers:
            src = self.partial.at[self.rows(index, self.two)]
            self.copies.append(self.remote(src, self.got_two.at[n], self.sems[2].at[n], self.sems[3].at[n], who))
            self.copies[-1].start()

    def gather_two(self, scale):
        self.wait()
        mine = self.rows(self.second.me, self.two)
        total = self.partial[mine].astype(F32)
        for n, _, _, _ in self.second.peers:
            total = total + self.got_two[n].astype(F32)
        self.whole[mine] = (total * scale).astype(BF)
        self.copies = []
        for n, who, _, _ in self.second.peers:
            block = self.whole.at[mine]
            self.copies.append(self.remote(block, block, self.sems[4].at[n], self.sems[5].at[n], who))
            self.copies[-1].start()

    def gather_one(self, core, partner):
        self.wait()
        home = self.rows(self.first.me, self.one, self.base)
        self.copies = []
        for n, who, _, _ in self.first.peers:
            src, dst = self.whole.at[: self.one], self.result.at[core, home]
            self.copies.append(self.remote(src, dst, self.sems[6].at[n], self.sems[7].at[n], who))
            self.copies[-1].start()
        self.result[core, home] = self.whole[: self.one]
        self.passed = []
        self.pass_on(core, partner, home, 0)

    def pass_on(self, core, partner, rows, n):
        block = self.result.at[core, rows]
        self.passed.append(self.remote(block, block, self.sems[8].at[n], self.sems[9].at[n], partner))
        self.passed[-1].start()

    def finish(self, core, partner, step):
        n, _, _, sender = self.first.peers[step]
        self.copies[step].wait()
        self.pass_on(core, partner, self.rows(sender, self.one, self.base), n)


class Group:
    def __init__(self, size, me, peers):
        self.size, self.me, self.peers = size, me, peers


class Halo:
    def __init__(self, refs):
        self.face, self.wall, self.edge, self.face_out, self.wall_out, self.diag_out, self.diag = refs


def kernel(dims, scale, *refs):
    (
        feat, occ, w1_hbm, bias, w2_hbm, cot, nbr, sx, sy,
        out_ref, gf_ref, gw_ref,
        w1, w2, mask, gate, sum0, sum1, fa0, fa1, fb0, fb1, za, zb, at, list_out, lists, gwo, gwm, crecv,
    ) = refs[:30]
    refs = refs[2:]
    halos = [Halo(refs[28 + 7 * i : 35 + 7 * i]) for i in range(4)]
    bufs_q, bufs_p = refs[56:60], refs[60:64]
    w_sem, halo_s, halo_r, core_s, core_r = refs[64:69]
    sems_q, sems_p = refs[69:79], refs[79:89]
    nx, ny, nzhi, nzlo, _ = dims
    nz = nzhi * nzlo
    ngx, ngy = nzlo * ny * 2, nx * nzhi
    gx, gy = lax.axis_index("gx"), lax.axis_index("gy")
    core = lax.rem(gx, 2)
    y = lax.rem(gx // 2, ny)
    z = lax.rem(gy, nzhi) * nzlo + gx // (2 * ny)
    x = gy // nzhi

    def device(px, py, pz, c):
        return (lax.rem(pz, nzlo) * (2 * ny) + py * 2 + c, px * nzhi + pz // nzlo)

    near_x = [lax.rem(gx + 1, ngx), lax.rem(gx + ngx - 1, ngx)]
    near_y = [lax.rem(gy + 1, ngy), lax.rem(gy + ngy - 1, ngy)]
    partner = device(x, y, z, 1 - core)
    in_plane = []
    for i in range(nx):
        for k in range(ny):
            if i or k:
                px, py = lax.rem(x + i, nx), lax.rem(y + k, ny)
                back = lax.rem(x + nx - i, nx) * ny + lax.rem(y + ny - k, ny)
                in_plane.append((i * ny + k, device(px, py, z, core), px * ny + py, back))
    plane = Group(nx * ny, x * ny + y, in_plane)
    in_line = [
        (d, device(x, y, lax.rem(z + d, nz), core), lax.rem(z + d, nz), lax.rem(z + nz - d, nz))
        for d in range(1, nz)
    ]
    line = Group(nz, z, in_line)

    barrier = pltpu.get_barrier_semaphore()
    greet = [(px, gy) for px in near_x] + [(gx, py) for py in near_y]
    greet += [(px, py) for px in near_x for py in near_y]
    greet += [peer[1] for peer in in_plane + in_line]
    for who in greet:
        pl.semaphore_signal(barrier, inc=1, device_id=who, device_id_type=MESH)
    load_w1 = pltpu.make_async_copy(w1_hbm, w1, w_sem.at[0])
    load_w2 = pltpu.make_async_copy(w2_hbm, w2, w_sem.at[1])
    load_w1.start()
    load_w2.start()

    for t in range(4):
        halves = []
        for b in range(2):
            live = (nbr[b, 13] != NONE).astype(F32)
            row = occ[b : b + 1, t * CH : (t + 1) * CH].astype(F32) * live
            halves.append(jnp.broadcast_to(row, (CH, CH)).T.reshape(16, EDGE, CH))
        mask[t * 16 : (t + 1) * 16] = jnp.stack(halves, 1).reshape(16, 16, CH)

    def masked_field(source, field):
        def layer(p, carry):
            part = pl.ds(p * EDGE, EDGE)
            rows = pl.ds(pl.multiple_of(p * PLANE, PLANE), PLANE)
            both = jnp.stack(
                [source[b, rows].astype(F32).reshape(EDGE, EDGE, CH) for b in range(2)], 1
            )
            field[part] = (both.reshape(EDGE, 16, CH) * mask[part]).astype(BF)
            return carry

        lax.fori_loop(0, EDGE, layer, 0)

    def remote(src, dst, send, recv, who):
        return pltpu.make_async_remote_copy(
            src_ref=src, dst_ref=dst, send_sem=send, recv_sem=recv, device_id=who, device_id_type=MESH
        )

    def own_faces(field, halo):
        for side in range(2):
            halo.face[side, NONE] = jnp.zeros((PLANE, CH), BF)
            halo.wall[side, 6] = jnp.zeros((PLANE, CH), BF)
            halo.edge[side, NONE] = jnp.zeros((16, CH), BF)
            end = (1 - side) * (EDGE - 1)
            faces = field[end * EDGE : (end + 1) * EDGE].astype(F32).reshape(EDGE, 2, EDGE, CH)
            walls = jnp.stack([field[p * EDGE + end].astype(F32) for p in range(EDGE)], 0)
            walls = walls.reshape(EDGE, 2, EDGE, CH)
            face = [faces[:, b].reshape(PLANE, CH) for b in range(2)]
            wall = [walls[:, b].reshape(PLANE, CH) for b in range(2)]
            for b in range(2):
                halo.face[side, b] = face[b].astype(BF)
                halo.wall[side, b] = wall[b].astype(BF)
                ends = jnp.concatenate([face[b][:EDGE], face[b][PLANE - EDGE :]], 0)
                halo.edge[side, b] = ends.astype(BF)
            chosen = []
            for r in range(2):
                for listed, picks in ((sx, face), (sy, wall)):
                    slot = listed[side, r]
                    low = jnp.where(slot == 0, picks[0], 0.0)
                    chosen.append(jnp.where(slot == 1, picks[1], low))
            for r in range(2):
                halo.face_out[side, r] = chosen[2 * r].astype(BF)
                halo.wall_out[side, r] = chosen[2 * r + 1].astype(BF)
            tops = jnp.concatenate([chosen[2 * r + 1][PLANE - EDGE :] for r in range(2)], 0)
            bottoms = jnp.concatenate([chosen[2 * r + 1][:EDGE] for r in range(2)], 0)
            halo.diag_out[0, side] = tops.astype(BF)
            halo.diag_out[1, side] = bottoms.astype(BF)

    def halo_copies(n, halo):
        copies = []

        def add(src, dst, who):
            m = len(copies)
            copies.append(remote(src, dst, halo_s.at[n, m], halo_r.at[n, m], who))

        for d in range(2):
            add(halo.wall_out.at[d], halo.wall.at[d, 2 + 2 * d : 4 + 2 * d], (gx, near_y[d]))
        for d in range(2):
            for e in range(2):
                add(halo.diag_out.at[d, e], halo.diag.at[d, e], (near_x[d], near_y[e]))
        for d in range(2):
            add(halo.face_out.at[d], halo.face.at[d, 6 + 6 * d : 8 + 6 * d], (near_x[d], gy))
        if n == 0:
            for d in range(2):
                add(list_out.at[d], lists.at[d], (near_x[d], gy))
        return copies

    def far_edges(halo):
        blank = jnp.zeros((EDGE, CH), F32)
        for r in range(2, 6):
            got = halo.wall[(r - 2) // 2, r].astype(F32)
            for side, part in ((0, got[PLANE - EDGE :]), (1, got[:EDGE])):
                pair = [blank, part] if r < 4 else [part, blank]
                halo.edge[side, r] = jnp.concatenate(pair, 0).astype(BF)
        for side in range(2):
            below = halo.diag[side, 0].astype(F32)
            above = halo.diag[side, 1].astype(F32)
            table = lists[side].astype(F32)
            for r in range(6):
                row = jnp.broadcast_to(table[r : r + 1], (EDGE, CH))
                low, high = blank, blank
                if r < 2:
                    got = halo.face[side, 6 + 6 * side + r].astype(F32)
                    low, high = got[:EDGE], got[PLANE - EDGE :]
                for i in range(2):
                    part = slice(i * EDGE, (i + 1) * EDGE)
                    high = jnp.where(row == 2.0 + i, below[part], high)
                    low = jnp.where(row == 4.0 + i, above[part], low)
                halo.edge[side, 6 + 6 * side + r] = jnp.concatenate([low, high], 0).astype(BF)

    def inner(field, z_ref, f):
        linked = [[(nbr[b, 12 + 2 * d] != NONE).astype(F32) for b in range(2)] for d in range(2)]

        def layer(p, carry):
            own = field[pl.ds(p * EDGE, EDGE)].astype(F32).reshape(EDGE, 2, EDGE, CH)
            near = [jnp.stack([own[:, 1] * linked[d][0], own[:, 0] * linked[d][1]], 1) for d in range(2)]
            for e, rows in enumerate(with_z(own, *near)):
                z_ref[f, p + 1, 1 : EDGE + 1, :, e * CH : (e + 1) * CH] = rows
            return carry

        lax.fori_loop(0, EDGE, layer, 0)

    def shell(halo, z_ref, f):
        far_edges(halo)

        def three(first, load):
            pick = lambda k: jnp.stack([load(nbr[b, k]).astype(F32) for b in range(2)], 1)
            return pick(first + 1), pick(first), pick(first + 2)

        middle = slice(1, EDGE + 1)
        for side in range(2):
            end = (EDGE + 1) * side
            faces = three(18 * side + 3, lambda r: halo.face[side, r].reshape(EDGE, EDGE, CH))
            for e, rows in enumerate(with_z(*faces)):
                z_ref[f, end, middle, :, e * CH : (e + 1) * CH] = rows
            walls = three(
                9 + 6 * side, lambda r: halo.wall[side, jnp.minimum(r, 6)].reshape(EDGE, EDGE, CH)
            )
            for e, rows in enumerate(with_z(*walls)):
                z_ref[f, middle, end, :, e * CH : (e + 1) * CH] = rows
            for up in range(2):
                low = (1 - up) * EDGE
                lines = three(
                    18 * side + 6 * up,
                    lambda r: halo.edge[side, r].astype(F32)[low : low + EDGE].reshape(1, EDGE, CH),
                )
                for e, rows in enumerate(with_z(*lines)):
                    z_ref[f, end, (EDGE + 1) * up, :, e * CH : (e + 1) * CH] = rows[0]

    half = 2
    tiles = half * EDGE
    steps = EDGE // half
    taps = [(a, c) for a in range(3) for c in range(3)]

    def columns(z_ref, f, m):
        parts = [
            z_ref[f, pl.ds(m * half + a, half), c : c + EDGE].reshape(tiles * 16, 3 * CH) for a, c in taps
        ]
        return jnp.concatenate(parts, 1)

    def conv(z_ref, f, m, w):
        return jnp.dot(columns(z_ref, f, m), w[...], preferred_element_type=F32)

    def conv_t(z_ref, f, m, w):
        turned = jnp.concatenate([w[(KVOL - 1 - k) * CH : (KVOL - k) * CH] for k in range(KVOL)], 1)
        return lax.dot_general(
            columns(z_ref, f, m), turned, (((1,), (1,)), ((), ())), preferred_element_type=F32
        )

    for d in range(2):
        index = lax.broadcasted_iota(jnp.int32, (16, CH), 0)
        table = jnp.full((16, CH), float(NONE), F32)
        for r in range(6):
            table = jnp.where(index == r, sx[d, r].astype(F32), table)
        list_out[d] = table.astype(BF)
    masked_field(feat, fa0)
    own_faces(fa0, halos[0])
    copies = [halo_copies(n, halos[n]) for n in range(4)]
    pl.semaphore_wait(barrier, len(greet))
    for copy in copies[0]:
        copy.start()
    masked_field(cot, fa1)
    own_faces(fa1, halos[1])
    for copy in copies[1]:
        copy.start()

    for f in range(2):
        for end in (0, EDGE + 1):
            za[f, end] = jnp.zeros((EDGE + 2, 16, 3 * CH), BF)
            za[f, 1 : EDGE + 1, end] = jnp.zeros((EDGE, 16, 3 * CH), BF)
    inner(fa0, za, 0)
    load_w1.wait()

    def inside_forward(m, carry):
        sum0[pl.ds(m * tiles, tiles)] = conv(za, 0, m, w1).reshape(tiles, 16, CH)
        return carry

    lax.fori_loop(0, steps, inside_forward, 0)
    inner(fa1, za, 1)
    load_w2.wait()

    def inside_backward(m, carry):
        sum1[pl.ds(m * tiles, tiles)] = conv_t(za, 1, m, w2).reshape(tiles, 16, CH)
        return carry

    lax.fori_loop(0, steps, inside_backward, 0)

    def sides(f, w, total, turned):
        def times(parts, which):
            left = jnp.concatenate([t.reshape(EDGE * 16, 3 * CH) for t in parts], 1)
            if turned:
                blocks = [
                    w[(KVOL - 1 - k) * CH : (KVOL - k) * CH]
                    for a, c in which
                    for k in range(9 * a + 3 * c, 9 * a + 3 * c + 3)
                ]
                right = jnp.concatenate(blocks, 1)
                got = lax.dot_general(left, right, (((1,), (1,)), ((), ())), preferred_element_type=F32)
            else:
                right = jnp.concatenate([w[(3 * a + c) * 3 * CH : (3 * a + c + 1) * 3 * CH] for a, c in which], 0)
                got = jnp.dot(left, right, preferred_element_type=F32)
            return got.reshape(EDGE, 16, CH)

        none = jnp.zeros((1, 16, 3 * CH), BF)
        for side in range(2):
            shell_at, inner_at, tap = (EDGE + 1) * side, (EDGE - 1) * side, 2 * side
            parts = [za[f, shell_at, c : c + EDGE] for c in range(3)]
            rows = slice(inner_at * EDGE, (inner_at + 1) * EDGE)
            total[rows] = total[rows] + times(parts, [(tap, c) for c in range(3)])
            wall = za[f, 1 : EDGE + 1, shell_at]
            parts = [
                jnp.concatenate([none, wall[: EDGE - 1]], 0),
                wall,
                jnp.concatenate([wall[1:], none], 0),
            ]
            more = times(parts, [(a, tap) for a in range(3)])
            for p in range(EDGE):
                total[p * EDGE + inner_at] = total[p * EDGE + inner_at] + more[p]

    for copy in copies[0]:
        copy.wait()
    shell(halos[0], za, 0)
    sides(0, w1, sum0, False)

    def forward_layer(m, carry):
        part = pl.ds(m * tiles, tiles)
        mk = mask[part].reshape(tiles * 16, CH)
        preact = sum0[part].reshape(tiles * 16, CH) + bias[...]
        hidden = (jnp.maximum(preact, 0.0) * mk).astype(BF)
        gate[part] = jnp.where(preact > 0, mk, 0.0).reshape(tiles, 16, CH)
        fb0[part] = hidden.reshape(tiles, 16, CH)
        at[1, m] = hidden.T
        return carry

    lax.fori_loop(0, steps, forward_layer, 0)
    own_faces(fb0, halos[2])
    for copy in copies[2]:
        copy.start()
    for copy in copies[1]:
        copy.wait()
    shell(halos[1], za, 1)
    sides(1, w2, sum1, True)

    def backward_layer(m, carry):
        part = pl.ds(m * tiles, tiles)
        grad = (sum1[part] * gate[part]).reshape(tiles * 16, CH).astype(BF)
        fb1[part] = grad.reshape(tiles, 16, CH)
        at[0, m] = grad.T
        return carry

    lax.fori_loop(0, steps, backward_layer, 0)
    own_faces(fb1, halos[3])
    for copy in copies[3]:
        copy.start()

    third = 9 * CH

    def weight_grad(which, a, dst, add=None):
        left = jnp.concatenate([at[which, i] for i in range(steps)], 1)
        first = which == 0
        pa = jnp.where(first, a, 2 - a)
        for c in range(3):
            pc = jnp.where(first, c, 2 - c)
            right = za[which, pl.ds(pa, EDGE), pl.ds(pc, EDGE)].reshape(PLANE * 16, 3 * CH)
            prod = jnp.dot(left, right, preferred_element_type=F32)
            for e in range(3):
                plain = prod[:, (2 - e) * CH : (3 - e) * CH]
                turned = prod[:, e * CH : (e + 1) * CH].T
                block = jnp.where(first, turned, plain)
                row = (9 * a + 3 * c + e) * CH
                if add is not None:
                    block = block + add[row : row + CH].astype(F32)
                dst[row : row + CH] = block.astype(BF)

    core_copies = [
        remote(
            gwo.at[a * third : (a + 1) * third],
            crecv.at[a * third : (a + 1) * third],
            core_s.at[a],
            core_r.at[a],
            partner,
        )
        for a in range(3)
    ]
    for a in range(3):
        weight_grad(1 - core, a, gwo)
        core_copies[a].start()
    part_q = Part(remote, gwm, gw_ref, 0, third, line, plane, bufs_q, sems_q)
    part_p = Part(remote, gwm, gw_ref, third, 2 * third, plane, line, bufs_p, sems_p)
    for a in range(3):
        core_copies[a].wait()
        weight_grad(core, a, gwm, crecv)
        if a == 0:
            part_q.scatter_one()
    part_p.scatter_one()
    inner(fb0, zb, 0)
    inner(fb1, zb, 1)
    part_q.scatter_two()
    part_p.scatter_two()

    def write(value, dst, m):
        rows = pl.ds(pl.multiple_of(m * tiles * EDGE, tiles * EDGE), tiles * EDGE)
        bricks = value.reshape(tiles, 2, EDGE, CH)
        for b in range(2):
            dst[b, rows] = bricks[:, b].reshape(tiles * EDGE, CH).astype(BF)

    def second_layer(m, carry):
        part = pl.ds(m * tiles, tiles)
        masked = fa0[part].astype(F32).reshape(tiles * 16, CH)
        write(conv(zb, 0, m, w2) * mask[part].reshape(tiles * 16, CH) + masked, out_ref, m)
        return carry

    for copy in copies[2]:
        copy.wait()
    shell(halos[2], zb, 0)
    lax.fori_loop(0, steps, second_layer, 0)
    part_q.gather_two(scale)
    part_p.gather_two(scale)

    def last_layer(m, carry):
        part = pl.ds(m * tiles, tiles)
        given = fa1[part].astype(F32).reshape(tiles * 16, CH)
        write(conv_t(zb, 1, m, w1) * mask[part].reshape(tiles * 16, CH) + given, gf_ref, m)
        return carry

    for copy in copies[3]:
        copy.wait()
    shell(halos[3], zb, 1)
    lax.fori_loop(0, steps, last_layer, 0)
    part_q.gather_one(core, partner)
    part_p.gather_one(core, partner)
    for step in range(max(plane.size, line.size) - 1):
        for part in (part_q, part_p):
            if step < part.first.size - 1:
                part.finish(core, partner, step)
    for part in (part_q, part_p):
        for copy in part.passed:
            copy.wait()


def convert(out_in, gf_in, gw_in, out, gf, one, two, wide, sems):
    copies = [pltpu.make_async_copy(out_in, out, sems.at[0]), pltpu.make_async_copy(gf_in, gf, sems.at[1])]
    for copy in copies:
        copy.start()
    cuts = 3
    size = gw_in.shape[1] // cuts
    for j, dst in enumerate((one, two)):
        for i in range(cuts):
            rows = pl.ds(i * size, size)
            wide[j, rows] = gw_in[j, rows].astype(F32)
            copies.append(pltpu.make_async_copy(wide.at[j, rows], dst.at[rows], sems.at[len(copies)]))
            copies[-1].start()
    for copy in copies:
        copy.wait()


def on_device(dims, features, occupied, weight_one, bias_one, weight_two, cotangent, neighbours, send_x, send_y):
    nx, ny, nzhi, nzlo, _ = dims
    nz, nxy = nzhi * nzlo, nx * ny
    slots, voxels, _ = features.shape
    scale = 1.0 / math.sqrt(slots * voxels * 2 * nxy * nz)
    vmem = pl.BlockSpec(memory_space=pltpu.VMEM)
    smem = pl.BlockSpec(memory_space=pltpu.SMEM)
    hbm = pl.BlockSpec(memory_space=pl.ANY)
    rows = KVOL * CH

    def halo():
        return [
            pltpu.VMEM((2, NONE + 1, PLANE, CH), BF),
            pltpu.VMEM((2, 7, PLANE, CH), BF),
            pltpu.VMEM((2, NONE + 1, 16, CH), BF),
            pltpu.VMEM((2, 2, PLANE, CH), BF),
            pltpu.VMEM((2, 2, PLANE, CH), BF),
            pltpu.VMEM((2, 2, 16, CH), BF),
            pltpu.VMEM((2, 2, 16, CH), BF),
        ]

    sem = lambda *shape: pltpu.SemaphoreType.DMA(shape)

    def part(total, n_one, n_two):
        one = total // n_one
        two = -(-one // (16 * n_two)) * 16
        bufs = [
            pltpu.VMEM((n_one, one, CH), BF),
            pltpu.VMEM((n_two * two, CH), BF),
            pltpu.VMEM((n_two, two, CH), BF),
            pltpu.VMEM((n_two * two, CH), BF),
        ]
        sizes = (n_one, n_one, n_two, n_two, n_two, n_two, n_one, n_one, n_one, n_one)
        return bufs, [sem(n) for n in sizes]

    bufs_q, sems_q = part(rows // 3, nz, nxy)
    bufs_p, sems_p = part(2 * rows // 3, nxy, nz)
    field = pltpu.VMEM((PLANE, 16, CH), BF)
    weight = pltpu.VMEM((rows, CH), BF)
    plain = pltpu.VMEM((PLANE, 16, CH), F32)
    padded = pltpu.VMEM((2, EDGE + 2, EDGE + 2, 16, 3 * CH), BF)
    lists = pltpu.VMEM((2, 16, CH), BF)
    made = pl.pallas_call(
        functools.partial(kernel, dims, scale),
        out_shape=(
            pltpu.VMEM(features.shape, BF),
            pltpu.VMEM(features.shape, BF),
            pltpu.VMEM((2, rows, CH), BF),
        ),
        in_specs=[vmem, vmem, hbm, vmem, hbm, vmem, smem, smem, smem],
        out_specs=(vmem, vmem, vmem),
        scratch_shapes=[
            weight, weight, plain, plain, plain, plain, field, field, field, field, padded, padded,
            pltpu.VMEM((2, 4, CH, 256), BF),
            lists, lists, weight, weight, weight,
            *halo(), *halo(), *halo(), *halo(),
            *bufs_q, *bufs_p,
            sem(2), sem(4, 10), sem(4, 10), sem(3), sem(3),
            *sems_q, *sems_p,
        ],
        compiler_params=pltpu.CompilerParams(
            collective_id=0, has_side_effects=True, vmem_limit_bytes=56 * 2**20
        ),
    )(
        features,
        occupied,
        weight_one.reshape(rows, CH),
        bias_one.reshape(1, CH),
        weight_two.reshape(rows, CH),
        cotangent,
        neighbours,
        send_x.reshape(2, -1),
        send_y.reshape(2, -1),
    )
    out, grad_features, one, two = pl.pallas_call(
        convert,
        out_shape=(
            jax.ShapeDtypeStruct(features.shape, BF),
            jax.ShapeDtypeStruct(features.shape, BF),
            jax.ShapeDtypeStruct((rows, CH), F32),
            jax.ShapeDtypeStruct((rows, CH), F32),
        ),
        in_specs=[vmem, vmem, vmem],
        out_specs=(hbm, hbm, hbm, hbm),
        scratch_shapes=[pltpu.VMEM((2, rows, CH), F32), sem(8)],
        compiler_params=pltpu.CompilerParams(vmem_limit_bytes=24 * 2**20),
    )(*made)
    return (out, grad_features, one.reshape(KVOL, CH, CH), two.reshape(KVOL, CH, CH))


def solution(mesh, dims=SLICE):
    in_specs = (
        P(("gx", "gy"), None, None),
        P(("gx", "gy"), None),
        P(),
        P(),
        P(),
        P(("gx", "gy"), None, None),
        P(("gx", "gy"), None),
        P(("gx", "gy"), None, None),
        P(("gx", "gy"), None, None),
    )
    out_specs = (P(("gx", "gy"), None, None), P(("gx", "gy"), None, None), P(), P())
    return jax.shard_map(
        functools.partial(on_device, dims), mesh=mesh, in_specs=in_specs, out_specs=out_specs, check_vma=False
    )
```

```python
import functools
import math

import jax
import jax.numpy as jnp
from jax import lax
from jax.experimental import pallas as pl
from jax.experimental.pallas import tpu as pltpu
from jax.sharding import PartitionSpec as P

EDGE = 8
KVOL = 27
CH = 128
PLANE = EDGE * EDGE
NONE = 18
BF = jnp.bfloat16
F32 = jnp.float32
MESH = pl.DeviceIdType.MESH
SLICE = (4, 4, 2, 4, 2)


def with_z(line, below, above):
    n = line.shape[0]
    flat = lambda t: t.reshape(n * 2, EDGE, CH)
    line, below, above = flat(line), flat(below), flat(above)
    level = lax.broadcasted_iota(jnp.int32, line.shape, 1)
    down = pltpu.roll(jnp.where(level == EDGE - 1, below, line), 1, 1)
    up = pltpu.roll(jnp.where(level == 0, above, line), EDGE - 1, 1)
    return [t.reshape(n, 2 * EDGE, CH).astype(BF) for t in (down, line, up)]


class Part:
    def __init__(self, remote, local, result, base, rows, first, second, bufs, sems):
        self.remote, self.local, self.result = remote, local, result
        self.base, self.first, self.second = base, first, second
        self.got_one, self.partial, self.got_two, self.whole = bufs
        self.sems = sems
        self.one = rows // first.size
        self.two = self.got_two.shape[1]

    def rows(self, index, n, base=0):
        return pl.ds(pl.multiple_of(base + index * n, 16), n)

    def scatter_one(self):
        self.copies = []
        for n, who, index, _ in self.first.peers:
            src = self.local.at[self.rows(index, self.one, self.base)]
            self.copies.append(self.remote(src, self.got_one.at[n], self.sems[0].at[n], self.sems[1].at[n], who))
            self.copies[-1].start()

    def wait(self):
        for copy in self.copies:
            copy.wait()

    def scatter_two(self):
        self.wait()

        def tile(t, carry):
            start = pl.multiple_of(t * 16, 16)
            own = pl.ds(pl.multiple_of(self.base + self.first.me * self.one + start, 16), 16)
            total = self.local[own].astype(F32)
            for n, _, _, _ in self.first.peers:
                total = total + self.got_one[n, pl.ds(start, 16)].astype(F32)
            self.partial[pl.ds(start, 16)] = total.astype(BF)
            return carry

        lax.fori_loop(0, self.one // 16, tile, 0)
        spare = self.partial.shape[0] - self.one
        if spare:
            self.partial[self.one :] = jnp.zeros((spare, CH), BF)
        self.copies = []
        for n, who, index, _ in self.second.peers:
            src = self.partial.at[self.rows(index, self.two)]
            self.copies.append(self.remote(src, self.got_two.at[n], self.sems[2].at[n], self.sems[3].at[n], who))
            self.copies[-1].start()

    def gather_two(self, scale):
        self.wait()
        mine = self.rows(self.second.me, self.two)
        total = self.partial[mine].astype(F32)
        for n, _, _, _ in self.second.peers:
            total = total + self.got_two[n].astype(F32)
        self.whole[mine] = (total * scale).astype(BF)
        self.copies = []
        for n, who, _, _ in self.second.peers:
            block = self.whole.at[mine]
            self.copies.append(self.remote(block, block, self.sems[4].at[n], self.sems[5].at[n], who))
            self.copies[-1].start()

    def gather_one(self, core, partner):
        self.wait()
        home = self.rows(self.first.me, self.one, self.base)
        self.copies = []
        for n, who, _, _ in self.first.peers:
            src, dst = self.whole.at[: self.one], self.result.at[core, home]
            self.copies.append(self.remote(src, dst, self.sems[6].at[n], self.sems[7].at[n], who))
            self.copies[-1].start()
        self.result[core, home] = self.whole[: self.one]
        self.passed = []
        self.pass_on(core, partner, home, 0)

    def pass_on(self, core, partner, rows, n):
        block = self.result.at[core, rows]
        self.passed.append(self.remote(block, block, self.sems[8].at[n], self.sems[9].at[n], partner))
        self.passed[-1].start()

    def finish(self, core, partner, step):
        n, _, _, sender = self.first.peers[step]
        self.copies[step].wait()
        self.pass_on(core, partner, self.rows(sender, self.one, self.base), n)


class Group:
    def __init__(self, size, me, peers):
        self.size, self.me, self.peers = size, me, peers


class Halo:
    def __init__(self, refs):
        self.face, self.wall, self.edge, self.face_out, self.wall_out, self.diag_out, self.diag = refs


def kernel(dims, scale, *refs):
    (
        feat, occ, w1_hbm, bias, w2_hbm, cot, nbr, sx, sy,
        out_ref, gf_ref, gw_ref,
        w1, w2, mask, gate, sum0, sum1, fa0, fa1, fb0, fb1, za, zb, at, list_out, lists, gwo, gwm, crecv,
    ) = refs[:30]
    refs = refs[2:]
    halos = [Halo(refs[28 + 7 * i : 35 + 7 * i]) for i in range(4)]
    bufs_q, bufs_p = refs[56:60], refs[60:64]
    w_sem, halo_s, halo_r, core_s, core_r = refs[64:69]
    sems_q, sems_p = refs[69:79], refs[79:89]
    nx, ny, nzhi, nzlo, _ = dims
    nz = nzhi * nzlo
    ngx, ngy = nzlo * ny * 2, nx * nzhi
    gx, gy = lax.axis_index("gx"), lax.axis_index("gy")
    core = lax.rem(gx, 2)
    y = lax.rem(gx // 2, ny)
    z = lax.rem(gy, nzhi) * nzlo + gx // (2 * ny)
    x = gy // nzhi

    def device(px, py, pz, c):
        return (lax.rem(pz, nzlo) * (2 * ny) + py * 2 + c, px * nzhi + pz // nzlo)

    near_x = [lax.rem(gx + 1, ngx), lax.rem(gx + ngx - 1, ngx)]
    near_y = [lax.rem(gy + 1, ngy), lax.rem(gy + ngy - 1, ngy)]
    partner = device(x, y, z, 1 - core)
    in_plane = []
    for i in range(nx):
        for k in range(ny):
            if i or k:
                px, py = lax.rem(x + i, nx), lax.rem(y + k, ny)
                back = lax.rem(x + nx - i, nx) * ny + lax.rem(y + ny - k, ny)
                in_plane.append((i * ny + k, device(px, py, z, core), px * ny + py, back))
    ring = lambda i, n: min(i, n - i)
    in_plane.sort(key=lambda p: -(ring(p[0] // ny, nx) + ring(p[0] % ny, ny)))
    plane = Group(nx * ny, x * ny + y, in_plane)
    in_line = [
        (d, device(x, y, lax.rem(z + d, nz), core), lax.rem(z + d, nz), lax.rem(z + nz - d, nz))
        for d in range(1, nz)
    ]
    in_line.sort(key=lambda p: -ring(p[0], nz))
    line = Group(nz, z, in_line)

    barrier = pltpu.get_barrier_semaphore()
    greet = [(px, gy) for px in near_x] + [(gx, py) for py in near_y]
    greet += [(px, py) for px in near_x for py in near_y]
    greet += [peer[1] for peer in in_plane + in_line]
    for who in greet:
        pl.semaphore_signal(barrier, inc=1, device_id=who, device_id_type=MESH)
    load_w1 = pltpu.make_async_copy(w1_hbm, w1, w_sem.at[0])
    load_w2 = pltpu.make_async_copy(w2_hbm, w2, w_sem.at[1])
    load_w1.start()
    load_w2.start()

    for t in range(4):
        halves = []
        for b in range(2):
            live = (nbr[b, 13] != NONE).astype(F32)
            row = occ[b : b + 1, t * CH : (t + 1) * CH].astype(F32) * live
            halves.append(jnp.broadcast_to(row, (CH, CH)).T.reshape(16, EDGE, CH))
        mask[t * 16 : (t + 1) * 16] = jnp.stack(halves, 1).reshape(16, 16, CH)

    def masked_field(source, field):
        def layer(p, carry):
            part = pl.ds(p * EDGE, EDGE)
            rows = pl.ds(pl.multiple_of(p * PLANE, PLANE), PLANE)
            both = jnp.stack(
                [source[b, rows].astype(F32).reshape(EDGE, EDGE, CH) for b in range(2)], 1
            )
            field[part] = (both.reshape(EDGE, 16, CH) * mask[part]).astype(BF)
            return carry

        lax.fori_loop(0, EDGE, layer, 0)

    def remote(src, dst, send, recv, who):
        return pltpu.make_async_remote_copy(
            src_ref=src, dst_ref=dst, send_sem=send, recv_sem=recv, device_id=who, device_id_type=MESH
        )

    def own_faces(field, halo):
        for side in range(2):
            halo.face[side, NONE] = jnp.zeros((PLANE, CH), BF)
            halo.wall[side, 6] = jnp.zeros((PLANE, CH), BF)
            halo.edge[side, NONE] = jnp.zeros((16, CH), BF)
            end = (1 - side) * (EDGE - 1)
            faces = field[end * EDGE : (end + 1) * EDGE].astype(F32).reshape(EDGE, 2, EDGE, CH)
            walls = jnp.stack([field[p * EDGE + end].astype(F32) for p in range(EDGE)], 0)
            walls = walls.reshape(EDGE, 2, EDGE, CH)
            face = [faces[:, b].reshape(PLANE, CH) for b in range(2)]
            wall = [walls[:, b].reshape(PLANE, CH) for b in range(2)]
            for b in range(2):
                halo.face[side, b] = face[b].astype(BF)
                halo.wall[side, b] = wall[b].astype(BF)
                ends = jnp.concatenate([face[b][:EDGE], face[b][PLANE - EDGE :]], 0)
                halo.edge[side, b] = ends.astype(BF)
            chosen = []
            for r in range(2):
                for listed, picks in ((sx, face), (sy, wall)):
                    slot = listed[side, r]
                    low = jnp.where(slot == 0, picks[0], 0.0)
                    chosen.append(jnp.where(slot == 1, picks[1], low))
            for r in range(2):
                halo.face_out[side, r] = chosen[2 * r].astype(BF)
                halo.wall_out[side, r] = chosen[2 * r + 1].astype(BF)
            tops = jnp.concatenate([chosen[2 * r + 1][PLANE - EDGE :] for r in range(2)], 0)
            bottoms = jnp.concatenate([chosen[2 * r + 1][:EDGE] for r in range(2)], 0)
            halo.diag_out[0, side] = tops.astype(BF)
            halo.diag_out[1, side] = bottoms.astype(BF)

    def halo_copies(n, halo):
        copies = []

        def add(src, dst, who):
            m = len(copies)
            copies.append(remote(src, dst, halo_s.at[n, m], halo_r.at[n, m], who))

        for d in range(2):
            add(halo.wall_out.at[d], halo.wall.at[d, 2 + 2 * d : 4 + 2 * d], (gx, near_y[d]))
        for d in range(2):
            for e in range(2):
                add(halo.diag_out.at[d, e], halo.diag.at[d, e], (near_x[d], near_y[e]))
        for d in range(2):
            add(halo.face_out.at[d], halo.face.at[d, 6 + 6 * d : 8 + 6 * d], (near_x[d], gy))
        if n == 0:
            for d in range(2):
                add(list_out.at[d], lists.at[d], (near_x[d], gy))
        return copies

    def far_edges(halo):
        blank = jnp.zeros((EDGE, CH), F32)
        for r in range(2, 6):
            got = halo.wall[(r - 2) // 2, r].astype(F32)
            for side, part in ((0, got[PLANE - EDGE :]), (1, got[:EDGE])):
                pair = [blank, part] if r < 4 else [part, blank]
                halo.edge[side, r] = jnp.concatenate(pair, 0).astype(BF)
        for side in range(2):
            below = halo.diag[side, 0].astype(F32)
            above = halo.diag[side, 1].astype(F32)
            table = lists[side].astype(F32)
            for r in range(6):
                row = jnp.broadcast_to(table[r : r + 1], (EDGE, CH))
                low, high = blank, blank
                if r < 2:
                    got = halo.face[side, 6 + 6 * side + r].astype(F32)
                    low, high = got[:EDGE], got[PLANE - EDGE :]
                for i in range(2):
                    part = slice(i * EDGE, (i + 1) * EDGE)
                    high = jnp.where(row == 2.0 + i, below[part], high)
                    low = jnp.where(row == 4.0 + i, above[part], low)
                halo.edge[side, 6 + 6 * side + r] = jnp.concatenate([low, high], 0).astype(BF)

    def inner(field, z_ref, f):
        linked = [[(nbr[b, 12 + 2 * d] != NONE).astype(F32) for b in range(2)] for d in range(2)]

        def layer(p, carry):
            own = field[pl.ds(p * EDGE, EDGE)].astype(F32).reshape(EDGE, 2, EDGE, CH)
            near = [jnp.stack([own[:, 1] * linked[d][0], own[:, 0] * linked[d][1]], 1) for d in range(2)]
            for e, rows in enumerate(with_z(own, *near)):
                z_ref[f, p + 1, 1 : EDGE + 1, :, e * CH : (e + 1) * CH] = rows
            return carry

        lax.fori_loop(0, EDGE, layer, 0)

    def shell(halo, z_ref, f):
        far_edges(halo)

        def three(first, load):
            pick = lambda k: jnp.stack([load(nbr[b, k]).astype(F32) for b in range(2)], 1)
            return pick(first + 1), pick(first), pick(first + 2)

        middle = slice(1, EDGE + 1)
        for side in range(2):
            end = (EDGE + 1) * side
            faces = three(18 * side + 3, lambda r: halo.face[side, r].reshape(EDGE, EDGE, CH))
            for e, rows in enumerate(with_z(*faces)):
                z_ref[f, end, middle, :, e * CH : (e + 1) * CH] = rows
            walls = three(
                9 + 6 * side, lambda r: halo.wall[side, jnp.minimum(r, 6)].reshape(EDGE, EDGE, CH)
            )
            for e, rows in enumerate(with_z(*walls)):
                z_ref[f, middle, end, :, e * CH : (e + 1) * CH] = rows
            for up in range(2):
                low = (1 - up) * EDGE
                lines = three(
                    18 * side + 6 * up,
                    lambda r: halo.edge[side, r].astype(F32)[low : low + EDGE].reshape(1, EDGE, CH),
                )
                for e, rows in enumerate(with_z(*lines)):
                    z_ref[f, end, (EDGE + 1) * up, :, e * CH : (e + 1) * CH] = rows[0]

    half = 2
    tiles = half * EDGE
    steps = EDGE // half
    taps = [(a, c) for a in range(3) for c in range(3)]

    def columns(z_ref, f, m):
        parts = [
            z_ref[f, pl.ds(m * half + a, half), c : c + EDGE].reshape(tiles * 16, 3 * CH) for a, c in taps
        ]
        return jnp.concatenate(parts, 1)

    def conv(z_ref, f, m, w):
        return jnp.dot(columns(z_ref, f, m), w[...], preferred_element_type=F32)

    def conv_t(z_ref, f, m, w):
        turned = jnp.concatenate([w[(KVOL - 1 - k) * CH : (KVOL - k) * CH] for k in range(KVOL)], 1)
        return lax.dot_general(
            columns(z_ref, f, m), turned, (((1,), (1,)), ((), ())), preferred_element_type=F32
        )

    for d in range(2):
        index = lax.broadcasted_iota(jnp.int32, (16, CH), 0)
        table = jnp.full((16, CH), float(NONE), F32)
        for r in range(6):
            table = jnp.where(index == r, sx[d, r].astype(F32), table)
        list_out[d] = table.astype(BF)
    masked_field(feat, fa0)
    own_faces(fa0, halos[0])
    copies = [halo_copies(n, halos[n]) for n in range(4)]
    pl.semaphore_wait(barrier, len(greet))
    for copy in copies[0]:
        copy.start()
    masked_field(cot, fa1)
    own_faces(fa1, halos[1])
    for copy in copies[1]:
        copy.start()

    for f in range(2):
        for end in (0, EDGE + 1):
            za[f, end] = jnp.zeros((EDGE + 2, 16, 3 * CH), BF)
            za[f, 1 : EDGE + 1, end] = jnp.zeros((EDGE, 16, 3 * CH), BF)
    inner(fa0, za, 0)
    load_w1.wait()

    def inside_forward(m, carry):
        sum0[pl.ds(m * tiles, tiles)] = conv(za, 0, m, w1).reshape(tiles, 16, CH)
        return carry

    lax.fori_loop(0, steps, inside_forward, 0)
    inner(fa1, za, 1)
    load_w2.wait()

    def inside_backward(m, carry):
        sum1[pl.ds(m * tiles, tiles)] = conv_t(za, 1, m, w2).reshape(tiles, 16, CH)
        return carry

    lax.fori_loop(0, steps, inside_backward, 0)

    def sides(f, w, total, turned):
        def times(parts, which):
            left = jnp.concatenate([t.reshape(EDGE * 16, 3 * CH) for t in parts], 1)
            if turned:
                blocks = [
                    w[(KVOL - 1 - k) * CH : (KVOL - k) * CH]
                    for a, c in which
                    for k in range(9 * a + 3 * c, 9 * a + 3 * c + 3)
                ]
                right = jnp.concatenate(blocks, 1)
                got = lax.dot_general(left, right, (((1,), (1,)), ((), ())), preferred_element_type=F32)
            else:
                right = jnp.concatenate([w[(3 * a + c) * 3 * CH : (3 * a + c + 1) * 3 * CH] for a, c in which], 0)
                got = jnp.dot(left, right, preferred_element_type=F32)
            return got.reshape(EDGE, 16, CH)

        none = jnp.zeros((1, 16, 3 * CH), BF)
        for side in range(2):
            shell_at, inner_at, tap = (EDGE + 1) * side, (EDGE - 1) * side, 2 * side
            parts = [za[f, shell_at, c : c + EDGE] for c in range(3)]
            rows = slice(inner_at * EDGE, (inner_at + 1) * EDGE)
            total[rows] = total[rows] + times(parts, [(tap, c) for c in range(3)])
            wall = za[f, 1 : EDGE + 1, shell_at]
            parts = [
                jnp.concatenate([none, wall[: EDGE - 1]], 0),
                wall,
                jnp.concatenate([wall[1:], none], 0),
            ]
            more = times(parts, [(a, tap) for a in range(3)])
            for p in range(EDGE):
                total[p * EDGE + inner_at] = total[p * EDGE + inner_at] + more[p]

    for copy in copies[0]:
        copy.wait()
    shell(halos[0], za, 0)
    sides(0, w1, sum0, False)

    def forward_layer(m, carry):
        part = pl.ds(m * tiles, tiles)
        mk = mask[part].reshape(tiles * 16, CH)
        preact = sum0[part].reshape(tiles * 16, CH) + bias[...]
        hidden = (jnp.maximum(preact, 0.0) * mk).astype(BF)
        gate[part] = jnp.where(preact > 0, mk, 0.0).reshape(tiles, 16, CH)
        fb0[part] = hidden.reshape(tiles, 16, CH)
        at[1, m] = hidden.T
        return carry

    lax.fori_loop(0, steps, forward_layer, 0)
    own_faces(fb0, halos[2])
    for copy in copies[2]:
        copy.start()
    for copy in copies[1]:
        copy.wait()
    shell(halos[1], za, 1)
    sides(1, w2, sum1, True)

    def backward_layer(m, carry):
        part = pl.ds(m * tiles, tiles)
        grad = (sum1[part] * gate[part]).reshape(tiles * 16, CH).astype(BF)
        fb1[part] = grad.reshape(tiles, 16, CH)
        at[0, m] = grad.T
        return carry

    lax.fori_loop(0, steps, backward_layer, 0)
    own_faces(fb1, halos[3])
    for copy in copies[3]:
        copy.start()

    third = 9 * CH

    def weight_grad(which, a, dst, add=None):
        left = jnp.concatenate([at[which, i] for i in range(steps)], 1)
        first = which == 0
        pa = jnp.where(first, a, 2 - a)
        for c in range(3):
            pc = jnp.where(first, c, 2 - c)
            right = za[which, pl.ds(pa, EDGE), pl.ds(pc, EDGE)].reshape(PLANE * 16, 3 * CH)
            prod = jnp.dot(left, right, preferred_element_type=F32)
            for e in range(3):
                plain = prod[:, (2 - e) * CH : (3 - e) * CH]
                turned = prod[:, e * CH : (e + 1) * CH].T
                block = jnp.where(first, turned, plain)
                row = (9 * a + 3 * c + e) * CH
                if add is not None:
                    block = block + add[row : row + CH].astype(F32)
                dst[row : row + CH] = block.astype(BF)

    core_copies = [
        remote(
            gwo.at[a * third : (a + 1) * third],
            crecv.at[a * third : (a + 1) * third],
            core_s.at[a],
            core_r.at[a],
            partner,
        )
        for a in range(3)
    ]
    for a in range(3):
        weight_grad(1 - core, a, gwo)
        core_copies[a].start()
    part_q = Part(remote, gwm, gw_ref, 0, third, line, plane, bufs_q, sems_q)
    part_p = Part(remote, gwm, gw_ref, third, 2 * third, plane, line, bufs_p, sems_p)
    for a in range(3):
        core_copies[a].wait()
        weight_grad(core, a, gwm, crecv)
        if a == 0:
            part_q.scatter_one()
    part_p.scatter_one()
    inner(fb0, zb, 0)
    inner(fb1, zb, 1)
    part_q.scatter_two()
    part_p.scatter_two()

    def write(value, dst, m):
        rows = pl.ds(pl.multiple_of(m * tiles * EDGE, tiles * EDGE), tiles * EDGE)
        bricks = value.reshape(tiles, 2, EDGE, CH)
        for b in range(2):
            dst[b, rows] = bricks[:, b].reshape(tiles * EDGE, CH).astype(BF)

    def second_layer(m, carry):
        part = pl.ds(m * tiles, tiles)
        masked = fa0[part].astype(F32).reshape(tiles * 16, CH)
        write(conv(zb, 0, m, w2) * mask[part].reshape(tiles * 16, CH) + masked, out_ref, m)
        return carry

    for copy in copies[2]:
        copy.wait()
    shell(halos[2], zb, 0)
    lax.fori_loop(0, steps, second_layer, 0)
    part_q.gather_two(scale)
    part_p.gather_two(scale)

    def last_layer(m, carry):
        part = pl.ds(m * tiles, tiles)
        given = fa1[part].astype(F32).reshape(tiles * 16, CH)
        write(conv_t(zb, 1, m, w1) * mask[part].reshape(tiles * 16, CH) + given, gf_ref, m)
        return carry

    for copy in copies[3]:
        copy.wait()
    shell(halos[3], zb, 1)
    lax.fori_loop(0, steps, last_layer, 0)
    part_q.gather_one(core, partner)
    part_p.gather_one(core, partner)
    for step in range(max(plane.size, line.size) - 1):
        for part in (part_q, part_p):
            if step < part.first.size - 1:
                part.finish(core, partner, part.first.size - 2 - step)
    for part in (part_q, part_p):
        for copy in part.passed:
            copy.wait()


def convert(out_in, gf_in, gw_in, out, gf, one, two, wide, sems):
    copies = [pltpu.make_async_copy(out_in, out, sems.at[0]), pltpu.make_async_copy(gf_in, gf, sems.at[1])]
    for copy in copies:
        copy.start()
    cuts = 3
    size = gw_in.shape[1] // cuts
    for j, dst in enumerate((one, two)):
        for i in range(cuts):
            rows = pl.ds(i * size, size)
            wide[j, rows] = gw_in[j, rows].astype(F32)
            copies.append(pltpu.make_async_copy(wide.at[j, rows], dst.at[rows], sems.at[len(copies)]))
            copies[-1].start()
    for copy in copies:
        copy.wait()


def on_device(dims, features, occupied, weight_one, bias_one, weight_two, cotangent, neighbours, send_x, send_y):
    nx, ny, nzhi, nzlo, _ = dims
    nz, nxy = nzhi * nzlo, nx * ny
    slots, voxels, _ = features.shape
    scale = 1.0 / math.sqrt(slots * voxels * 2 * nxy * nz)
    vmem = pl.BlockSpec(memory_space=pltpu.VMEM)
    smem = pl.BlockSpec(memory_space=pltpu.SMEM)
    hbm = pl.BlockSpec(memory_space=pl.ANY)
    rows = KVOL * CH

    def halo():
        return [
            pltpu.VMEM((2, NONE + 1, PLANE, CH), BF),
            pltpu.VMEM((2, 7, PLANE, CH), BF),
            pltpu.VMEM((2, NONE + 1, 16, CH), BF),
            pltpu.VMEM((2, 2, PLANE, CH), BF),
            pltpu.VMEM((2, 2, PLANE, CH), BF),
            pltpu.VMEM((2, 2, 16, CH), BF),
            pltpu.VMEM((2, 2, 16, CH), BF),
        ]

    sem = lambda *shape: pltpu.SemaphoreType.DMA(shape)

    def part(total, n_one, n_two):
        one = total // n_one
        two = -(-one // (16 * n_two)) * 16
        bufs = [
            pltpu.VMEM((n_one, one, CH), BF),
            pltpu.VMEM((n_two * two, CH), BF),
            pltpu.VMEM((n_two, two, CH), BF),
            pltpu.VMEM((n_two * two, CH), BF),
        ]
        sizes = (n_one, n_one, n_two, n_two, n_two, n_two, n_one, n_one, n_one, n_one)
        return bufs, [sem(n) for n in sizes]

    bufs_q, sems_q = part(rows // 3, nz, nxy)
    bufs_p, sems_p = part(2 * rows // 3, nxy, nz)
    field = pltpu.VMEM((PLANE, 16, CH), BF)
    weight = pltpu.VMEM((rows, CH), BF)
    plain = pltpu.VMEM((PLANE, 16, CH), F32)
    padded = pltpu.VMEM((2, EDGE + 2, EDGE + 2, 16, 3 * CH), BF)
    lists = pltpu.VMEM((2, 16, CH), BF)
    made = pl.pallas_call(
        functools.partial(kernel, dims, scale),
        out_shape=(
            pltpu.VMEM(features.shape, BF),
            pltpu.VMEM(features.shape, BF),
            pltpu.VMEM((2, rows, CH), BF),
        ),
        in_specs=[vmem, vmem, hbm, vmem, hbm, vmem, smem, smem, smem],
        out_specs=(vmem, vmem, vmem),
        scratch_shapes=[
            weight, weight, plain, plain, plain, plain, field, field, field, field, padded, padded,
            pltpu.VMEM((2, 4, CH, 256), BF),
            lists, lists, weight, weight, weight,
            *halo(), *halo(), *halo(), *halo(),
            *bufs_q, *bufs_p,
            sem(2), sem(4, 10), sem(4, 10), sem(3), sem(3),
            *sems_q, *sems_p,
        ],
        compiler_params=pltpu.CompilerParams(
            collective_id=0, has_side_effects=True, vmem_limit_bytes=56 * 2**20
        ),
    )(
        features,
        occupied,
        weight_one.reshape(rows, CH),
        bias_one.reshape(1, CH),
        weight_two.reshape(rows, CH),
        cotangent,
        neighbours,
        send_x.reshape(2, -1),
        send_y.reshape(2, -1),
    )
    out, grad_features, one, two = pl.pallas_call(
        convert,
        out_shape=(
            jax.ShapeDtypeStruct(features.shape, BF),
            jax.ShapeDtypeStruct(features.shape, BF),
            jax.ShapeDtypeStruct((rows, CH), F32),
            jax.ShapeDtypeStruct((rows, CH), F32),
        ),
        in_specs=[vmem, vmem, vmem],
        out_specs=(hbm, hbm, hbm, hbm),
        scratch_shapes=[pltpu.VMEM((2, rows, CH), F32), sem(8)],
        compiler_params=pltpu.CompilerParams(vmem_limit_bytes=24 * 2**20),
    )(*made)
    return (out, grad_features, one.reshape(KVOL, CH, CH), two.reshape(KVOL, CH, CH))


def solution(mesh, dims=SLICE):
    in_specs = (
        P(("gx", "gy"), None, None),
        P(("gx", "gy"), None),
        P(),
        P(),
        P(),
        P(("gx", "gy"), None, None),
        P(("gx", "gy"), None),
        P(("gx", "gy"), None, None),
        P(("gx", "gy"), None, None),
    )
    out_specs = (P(("gx", "gy"), None, None), P(("gx", "gy"), None, None), P(), P())
    return jax.shard_map(
        functools.partial(on_device, dims), mesh=mesh, in_specs=in_specs, out_specs=out_specs, check_vma=False
    )
```

```python
import functools
import math

import jax
import jax.numpy as jnp
from jax import lax
from jax.experimental import pallas as pl
from jax.experimental.pallas import tpu as pltpu
from jax.sharding import PartitionSpec as P

EDGE = 8
KVOL = 27
CH = 128
PLANE = EDGE * EDGE
NONE = 18
BF = jnp.bfloat16
F32 = jnp.float32
MESH = pl.DeviceIdType.MESH
SLICE = (4, 4, 2, 4, 2)


def with_z(line, below, above):
    n = line.shape[0]
    flat = lambda t: t.reshape(n * 2, EDGE, CH)
    line, below, above = flat(line), flat(below), flat(above)
    level = lax.broadcasted_iota(jnp.int32, line.shape, 1)
    down = pltpu.roll(jnp.where(level == EDGE - 1, below, line), 1, 1)
    up = pltpu.roll(jnp.where(level == 0, above, line), EDGE - 1, 1)
    return [t.reshape(n, 2 * EDGE, CH).astype(BF) for t in (down, line, up)]


class Part:
    def __init__(self, remote, local, result, base, rows, first, second, bufs, sems):
        self.remote, self.local, self.result = remote, local, result
        self.base, self.first, self.second = base, first, second
        self.got_one, self.partial, self.got_two, self.whole = bufs
        self.sems = sems
        self.one = rows // first.size
        self.two = self.got_two.shape[1]

    def rows(self, index, n, base=0):
        return pl.ds(pl.multiple_of(base + index * n, 16), n)

    def scatter_one(self):
        self.copies = []
        for n, who, index, _ in self.first.peers:
            src = self.local.at[self.rows(index, self.one, self.base)]
            self.copies.append(self.remote(src, self.got_one.at[n], self.sems[0].at[n], self.sems[1].at[n], who))
            self.copies[-1].start()

    def wait(self):
        for copy in self.copies:
            copy.wait()

    def scatter_two(self):
        self.wait()

        def tile(t, carry):
            start = pl.multiple_of(t * 16, 16)
            own = pl.ds(pl.multiple_of(self.base + self.first.me * self.one + start, 16), 16)
            total = self.local[own].astype(F32)
            for n, _, _, _ in self.first.peers:
                total = total + self.got_one[n, pl.ds(start, 16)].astype(F32)
            self.partial[pl.ds(start, 16)] = total.astype(BF)
            return carry

        lax.fori_loop(0, self.one // 16, tile, 0)
        spare = self.partial.shape[0] - self.one
        if spare:
            self.partial[self.one :] = jnp.zeros((spare, CH), BF)
        self.copies = []
        for n, who, index, _ in self.second.peers:
            src = self.partial.at[self.rows(index, self.two)]
            self.copies.append(self.remote(src, self.got_two.at[n], self.sems[2].at[n], self.sems[3].at[n], who))
            self.copies[-1].start()

    def gather_two(self, scale):
        self.wait()
        mine = self.rows(self.second.me, self.two)
        total = self.partial[mine].astype(F32)
        for n, _, _, _ in self.second.peers:
            total = total + self.got_two[n].astype(F32)
        self.whole[mine] = (total * scale).astype(BF)
        self.copies = []
        for n, who, _, _ in self.second.peers:
            block = self.whole.at[mine]
            self.copies.append(self.remote(block, block, self.sems[4].at[n], self.sems[5].at[n], who))
            self.copies[-1].start()

    def gather_one(self, core, partner):
        self.wait()
        home = self.rows(self.first.me, self.one, self.base)
        self.copies = []
        for n, who, _, _ in self.first.peers:
            src, dst = self.whole.at[: self.one], self.result.at[core, home]
            self.copies.append(self.remote(src, dst, self.sems[6].at[n], self.sems[7].at[n], who))
            self.copies[-1].start()
        self.result[core, home] = self.whole[: self.one]
        self.passed = []
        self.pass_on(core, partner, home, 0)

    def pass_on(self, core, partner, rows, n):
        block = self.result.at[core, rows]
        self.passed.append(self.remote(block, block, self.sems[8].at[n], self.sems[9].at[n], partner))
        self.passed[-1].start()

    def finish(self, core, partner, step):
        n, _, _, sender = self.first.peers[step]
        self.copies[step].wait()
        self.pass_on(core, partner, self.rows(sender, self.one, self.base), n)


class Group:
    def __init__(self, size, me, peers):
        self.size, self.me, self.peers = size, me, peers


class Halo:
    def __init__(self, refs):
        self.face, self.wall, self.edge, self.face_out, self.wall_out, self.diag_out, self.diag = refs


def kernel(dims, scale, *refs):
    (
        feat, occ, w1_hbm, bias, w2_hbm, cot, nbr, sx, sy,
        out_ref, gf_ref, gw_ref,
        w1, w2, mask, gate, sum0, sum1, fa0, fa1, fb0, fb1, za, zb, at, list_out, lists, gwo, gwm, crecv,
    ) = refs[:30]
    refs = refs[2:]
    halos = [Halo(refs[28 + 7 * i : 35 + 7 * i]) for i in range(4)]
    bufs_q, bufs_p = refs[56:60], refs[60:64]
    w_sem, halo_s, halo_r, core_s, core_r = refs[64:69]
    sems_q, sems_p = refs[69:79], refs[79:89]
    early = refs[89]
    nx, ny, nzhi, nzlo, _ = dims
    nz = nzhi * nzlo
    ngx, ngy = nzlo * ny * 2, nx * nzhi
    gx, gy = lax.axis_index("gx"), lax.axis_index("gy")
    core = lax.rem(gx, 2)
    y = lax.rem(gx // 2, ny)
    z = lax.rem(gy, nzhi) * nzlo + gx // (2 * ny)
    x = gy // nzhi

    def device(px, py, pz, c):
        return (lax.rem(pz, nzlo) * (2 * ny) + py * 2 + c, px * nzhi + pz // nzlo)

    near_x = [lax.rem(gx + 1, ngx), lax.rem(gx + ngx - 1, ngx)]
    near_y = [lax.rem(gy + 1, ngy), lax.rem(gy + ngy - 1, ngy)]
    partner = device(x, y, z, 1 - core)
    in_plane = []
    for i in range(nx):
        for k in range(ny):
            if i or k:
                px, py = lax.rem(x + i, nx), lax.rem(y + k, ny)
                back = lax.rem(x + nx - i, nx) * ny + lax.rem(y + ny - k, ny)
                in_plane.append((i * ny + k, device(px, py, z, core), px * ny + py, back))
    ring = lambda i, n: min(i, n - i)
    in_plane.sort(key=lambda p: -(ring(p[0] // ny, nx) + ring(p[0] % ny, ny)))
    plane = Group(nx * ny, x * ny + y, in_plane)
    in_line = [
        (d, device(x, y, lax.rem(z + d, nz), core), lax.rem(z + d, nz), lax.rem(z + nz - d, nz))
        for d in range(1, nz)
    ]
    in_line.sort(key=lambda p: -ring(p[0], nz))
    line = Group(nz, z, in_line)

    barrier = pltpu.get_barrier_semaphore()
    greet = [(px, gy) for px in near_x] + [(gx, py) for py in near_y]
    greet += [(px, py) for px in near_x for py in near_y]
    greet += [peer[1] for peer in in_plane + in_line]
    for who in greet:
        pl.semaphore_signal(barrier, inc=1, device_id=who, device_id_type=MESH)
    load_w1 = pltpu.make_async_copy(w1_hbm, w1, w_sem.at[0])
    load_w2 = pltpu.make_async_copy(w2_hbm, w2, w_sem.at[1])
    load_w1.start()
    load_w2.start()

    for t in range(4):
        halves = []
        for b in range(2):
            live = (nbr[b, 13] != NONE).astype(F32)
            row = occ[b : b + 1, t * CH : (t + 1) * CH].astype(F32) * live
            halves.append(jnp.broadcast_to(row, (CH, CH)).T.reshape(16, EDGE, CH))
        mask[t * 16 : (t + 1) * 16] = jnp.stack(halves, 1).reshape(16, 16, CH)

    def masked_field(source, field):
        def layer(p, carry):
            part = pl.ds(p * EDGE, EDGE)
            rows = pl.ds(pl.multiple_of(p * PLANE, PLANE), PLANE)
            both = jnp.stack(
                [source[b, rows].astype(F32).reshape(EDGE, EDGE, CH) for b in range(2)], 1
            )
            field[part] = (both.reshape(EDGE, 16, CH) * mask[part]).astype(BF)
            return carry

        lax.fori_loop(0, EDGE, layer, 0)

    def remote(src, dst, send, recv, who):
        return pltpu.make_async_remote_copy(
            src_ref=src, dst_ref=dst, send_sem=send, recv_sem=recv, device_id=who, device_id_type=MESH
        )

    def own_faces(field, halo):
        for side in range(2):
            halo.face[side, NONE] = jnp.zeros((PLANE, CH), BF)
            halo.wall[side, 6] = jnp.zeros((PLANE, CH), BF)
            halo.edge[side, NONE] = jnp.zeros((16, CH), BF)
            end = (1 - side) * (EDGE - 1)
            faces = field[end * EDGE : (end + 1) * EDGE].astype(F32).reshape(EDGE, 2, EDGE, CH)
            walls = jnp.stack([field[p * EDGE + end].astype(F32) for p in range(EDGE)], 0)
            walls = walls.reshape(EDGE, 2, EDGE, CH)
            face = [faces[:, b].reshape(PLANE, CH) for b in range(2)]
            wall = [walls[:, b].reshape(PLANE, CH) for b in range(2)]
            for b in range(2):
                halo.face[side, b] = face[b].astype(BF)
                halo.wall[side, b] = wall[b].astype(BF)
                ends = jnp.concatenate([face[b][:EDGE], face[b][PLANE - EDGE :]], 0)
                halo.edge[side, b] = ends.astype(BF)
            chosen = []
            for r in range(2):
                for listed, picks in ((sx, face), (sy, wall)):
                    slot = listed[side, r]
                    low = jnp.where(slot == 0, picks[0], 0.0)
                    chosen.append(jnp.where(slot == 1, picks[1], low))
            for r in range(2):
                halo.face_out[side, r] = chosen[2 * r].astype(BF)
                halo.wall_out[side, r] = chosen[2 * r + 1].astype(BF)
            tops = jnp.concatenate([chosen[2 * r + 1][PLANE - EDGE :] for r in range(2)], 0)
            bottoms = jnp.concatenate([chosen[2 * r + 1][:EDGE] for r in range(2)], 0)
            halo.diag_out[0, side] = tops.astype(BF)
            halo.diag_out[1, side] = bottoms.astype(BF)

    def halo_copies(n, halo):
        copies = []

        def add(src, dst, who):
            m = len(copies)
            copies.append(remote(src, dst, halo_s.at[n, m], halo_r.at[n, m], who))

        for d in range(2):
            for e in range(2):
                add(halo.diag_out.at[d, e], halo.diag.at[d, e], (near_x[d], near_y[e]))
        for d in range(2):
            add(halo.wall_out.at[d], halo.wall.at[d, 2 + 2 * d : 4 + 2 * d], (gx, near_y[d]))
        for d in range(2):
            add(halo.face_out.at[d], halo.face.at[d, 6 + 6 * d : 8 + 6 * d], (near_x[d], gy))
        if n == 0:
            for d in range(2):
                add(list_out.at[d], lists.at[d], (near_x[d], gy))
        return copies

    def far_edges(halo):
        blank = jnp.zeros((EDGE, CH), F32)
        for r in range(2, 6):
            got = halo.wall[(r - 2) // 2, r].astype(F32)
            for side, part in ((0, got[PLANE - EDGE :]), (1, got[:EDGE])):
                pair = [blank, part] if r < 4 else [part, blank]
                halo.edge[side, r] = jnp.concatenate(pair, 0).astype(BF)
        for side in range(2):
            below = halo.diag[side, 0].astype(F32)
            above = halo.diag[side, 1].astype(F32)
            table = lists[side].astype(F32)
            for r in range(6):
                row = jnp.broadcast_to(table[r : r + 1], (EDGE, CH))
                low, high = blank, blank
                if r < 2:
                    got = halo.face[side, 6 + 6 * side + r].astype(F32)
                    low, high = got[:EDGE], got[PLANE - EDGE :]
                for i in range(2):
                    part = slice(i * EDGE, (i + 1) * EDGE)
                    high = jnp.where(row == 2.0 + i, below[part], high)
                    low = jnp.where(row == 4.0 + i, above[part], low)
                halo.edge[side, 6 + 6 * side + r] = jnp.concatenate([low, high], 0).astype(BF)

    def inner(field, z_ref, f):
        linked = [[(nbr[b, 12 + 2 * d] != NONE).astype(F32) for b in range(2)] for d in range(2)]

        def layer(p, carry):
            own = field[pl.ds(p * EDGE, EDGE)].astype(F32).reshape(EDGE, 2, EDGE, CH)
            near = [jnp.stack([own[:, 1] * linked[d][0], own[:, 0] * linked[d][1]], 1) for d in range(2)]
            for e, rows in enumerate(with_z(own, *near)):
                z_ref[f, p + 1, 1 : EDGE + 1, :, e * CH : (e + 1) * CH] = rows
            return carry

        lax.fori_loop(0, EDGE, layer, 0)

    def shell(halo, z_ref, f):
        far_edges(halo)

        def three(first, load):
            pick = lambda k: jnp.stack([load(nbr[b, k]).astype(F32) for b in range(2)], 1)
            return pick(first + 1), pick(first), pick(first + 2)

        middle = slice(1, EDGE + 1)
        for side in range(2):
            end = (EDGE + 1) * side
            faces = three(18 * side + 3, lambda r: halo.face[side, r].reshape(EDGE, EDGE, CH))
            for e, rows in enumerate(with_z(*faces)):
                z_ref[f, end, middle, :, e * CH : (e + 1) * CH] = rows
            walls = three(
                9 + 6 * side, lambda r: halo.wall[side, jnp.minimum(r, 6)].reshape(EDGE, EDGE, CH)
            )
            for e, rows in enumerate(with_z(*walls)):
                z_ref[f, middle, end, :, e * CH : (e + 1) * CH] = rows
            for up in range(2):
                low = (1 - up) * EDGE
                lines = three(
                    18 * side + 6 * up,
                    lambda r: halo.edge[side, r].astype(F32)[low : low + EDGE].reshape(1, EDGE, CH),
                )
                for e, rows in enumerate(with_z(*lines)):
                    z_ref[f, end, (EDGE + 1) * up, :, e * CH : (e + 1) * CH] = rows[0]

    half = 2
    tiles = half * EDGE
    steps = EDGE // half
    taps = [(a, c) for a in range(3) for c in range(3)]

    def columns(z_ref, f, m):
        parts = [
            z_ref[f, pl.ds(m * half + a, half), c : c + EDGE].reshape(tiles * 16, 3 * CH) for a, c in taps
        ]
        return jnp.concatenate(parts, 1)

    def conv(z_ref, f, m, w):
        return jnp.dot(columns(z_ref, f, m), w[...], preferred_element_type=F32)

    def conv_t(z_ref, f, m, w):
        turned = jnp.concatenate([w[(KVOL - 1 - k) * CH : (KVOL - k) * CH] for k in range(KVOL)], 1)
        return lax.dot_general(
            columns(z_ref, f, m), turned, (((1,), (1,)), ((), ())), preferred_element_type=F32
        )

    for d in range(2):
        index = lax.broadcasted_iota(jnp.int32, (16, CH), 0)
        table = jnp.full((16, CH), float(NONE), F32)
        for r in range(6):
            table = jnp.where(index == r, sx[d, r].astype(F32), table)
        list_out[d] = table.astype(BF)
    masked_field(feat, fa0)
    own_faces(fa0, halos[0])
    copies = [halo_copies(n, halos[n]) for n in range(4)]
    pl.semaphore_wait(barrier, len(greet))
    for copy in copies[0]:
        copy.start()
    masked_field(cot, fa1)
    own_faces(fa1, halos[1])
    for copy in copies[1]:
        copy.start()

    for f in range(2):
        for end in (0, EDGE + 1):
            za[f, end] = jnp.zeros((EDGE + 2, 16, 3 * CH), BF)
            za[f, 1 : EDGE + 1, end] = jnp.zeros((EDGE, 16, 3 * CH), BF)
    inner(fa0, za, 0)
    load_w1.wait()

    def inside_forward(m, carry):
        sum0[pl.ds(m * tiles, tiles)] = conv(za, 0, m, w1).reshape(tiles, 16, CH)
        return carry

    lax.fori_loop(0, steps, inside_forward, 0)
    inner(fa1, za, 1)
    load_w2.wait()

    def inside_backward(m, carry):
        sum1[pl.ds(m * tiles, tiles)] = conv_t(za, 1, m, w2).reshape(tiles, 16, CH)
        return carry

    lax.fori_loop(0, steps, inside_backward, 0)

    def sides(f, w, total, turned):
        def times(parts, which):
            left = jnp.concatenate([t.reshape(EDGE * 16, 3 * CH) for t in parts], 1)
            if turned:
                blocks = [
                    w[(KVOL - 1 - k) * CH : (KVOL - k) * CH]
                    for a, c in which
                    for k in range(9 * a + 3 * c, 9 * a + 3 * c + 3)
                ]
                right = jnp.concatenate(blocks, 1)
                got = lax.dot_general(left, right, (((1,), (1,)), ((), ())), preferred_element_type=F32)
            else:
                right = jnp.concatenate([w[(3 * a + c) * 3 * CH : (3 * a + c + 1) * 3 * CH] for a, c in which], 0)
                got = jnp.dot(left, right, preferred_element_type=F32)
            return got.reshape(EDGE, 16, CH)

        none = jnp.zeros((1, 16, 3 * CH), BF)
        for side in range(2):
            shell_at, inner_at, tap = (EDGE + 1) * side, (EDGE - 1) * side, 2 * side
            parts = [za[f, shell_at, c : c + EDGE] for c in range(3)]
            rows = slice(inner_at * EDGE, (inner_at + 1) * EDGE)
            total[rows] = total[rows] + times(parts, [(tap, c) for c in range(3)])
            wall = za[f, 1 : EDGE + 1, shell_at]
            parts = [
                jnp.concatenate([none, wall[: EDGE - 1]], 0),
                wall,
                jnp.concatenate([wall[1:], none], 0),
            ]
            more = times(parts, [(a, tap) for a in range(3)])
            for p in range(EDGE):
                total[p * EDGE + inner_at] = total[p * EDGE + inner_at] + more[p]

    for copy in copies[0]:
        copy.wait()
    shell(halos[0], za, 0)
    sides(0, w1, sum0, False)

    def forward_layer(m, carry):
        part = pl.ds(m * tiles, tiles)
        mk = mask[part].reshape(tiles * 16, CH)
        preact = sum0[part].reshape(tiles * 16, CH) + bias[...]
        hidden = (jnp.maximum(preact, 0.0) * mk).astype(BF)
        gate[part] = jnp.where(preact > 0, mk, 0.0).reshape(tiles, 16, CH)
        fb0[part] = hidden.reshape(tiles, 16, CH)
        at[1, m] = hidden.T
        return carry

    lax.fori_loop(0, steps, forward_layer, 0)
    own_faces(fb0, halos[2])
    for copy in copies[2]:
        copy.start()
    for copy in copies[1]:
        copy.wait()
    shell(halos[1], za, 1)
    sides(1, w2, sum1, True)

    def backward_layer(m, carry):
        part = pl.ds(m * tiles, tiles)
        grad = (sum1[part] * gate[part]).reshape(tiles * 16, CH).astype(BF)
        fb1[part] = grad.reshape(tiles, 16, CH)
        at[0, m] = grad.T
        return carry

    lax.fori_loop(0, steps, backward_layer, 0)
    own_faces(fb1, halos[3])
    for copy in copies[3]:
        copy.start()

    third = 9 * CH

    def weight_grad(which, a, dst, add=None):
        left = jnp.concatenate([at[which, i] for i in range(steps)], 1)
        first = which == 0
        pa = jnp.where(first, a, 2 - a)
        for c in range(3):
            pc = jnp.where(first, c, 2 - c)
            right = za[which, pl.ds(pa, EDGE), pl.ds(pc, EDGE)].reshape(PLANE * 16, 3 * CH)
            prod = jnp.dot(left, right, preferred_element_type=F32)
            for e in range(3):
                plain = prod[:, (2 - e) * CH : (3 - e) * CH]
                turned = prod[:, e * CH : (e + 1) * CH].T
                block = jnp.where(first, turned, plain)
                row = (9 * a + 3 * c + e) * CH
                if add is not None:
                    block = block + add[row : row + CH].astype(F32)
                dst[row : row + CH] = block.astype(dst.dtype)

    core_copies = [
        remote(
            gwo.at[a * third : (a + 1) * third],
            crecv.at[a * third : (a + 1) * third],
            core_s.at[a],
            core_r.at[a],
            partner,
        )
        for a in range(3)
    ]
    weight_grad(1 - core, 0, gwo)
    core_copies[0].start()
    weight_grad(core, 0, early)
    for a in range(1, 3):
        weight_grad(1 - core, a, gwo)
        core_copies[a].start()
    part_q = Part(remote, gwm, gw_ref, 0, third, line, plane, bufs_q, sems_q)
    part_p = Part(remote, gwm, gw_ref, third, 2 * third, plane, line, bufs_p, sems_p)
    core_copies[0].wait()

    def add_first(t, carry):
        rows = pl.ds(pl.multiple_of(t * CH, CH), CH)
        gwm[rows] = (early[rows] + crecv[rows].astype(F32)).astype(BF)
        return carry

    lax.fori_loop(0, 9, add_first, 0)
    part_q.scatter_one()
    for a in range(1, 3):
        core_copies[a].wait()
        weight_grad(core, a, gwm, crecv)
    part_p.scatter_one()
    inner(fb0, zb, 0)
    inner(fb1, zb, 1)
    part_q.scatter_two()
    part_p.scatter_two()

    def write(value, dst, m):
        rows = pl.ds(pl.multiple_of(m * tiles * EDGE, tiles * EDGE), tiles * EDGE)
        bricks = value.reshape(tiles, 2, EDGE, CH)
        for b in range(2):
            dst[b, rows] = bricks[:, b].reshape(tiles * EDGE, CH).astype(BF)

    def second_layer(m, carry):
        part = pl.ds(m * tiles, tiles)
        masked = fa0[part].astype(F32).reshape(tiles * 16, CH)
        write(conv(zb, 0, m, w2) * mask[part].reshape(tiles * 16, CH) + masked, out_ref, m)
        return carry

    for copy in copies[2]:
        copy.wait()
    shell(halos[2], zb, 0)
    lax.fori_loop(0, steps, second_layer, 0)
    part_q.gather_two(scale)
    part_p.gather_two(scale)

    def last_layer(m, carry):
        part = pl.ds(m * tiles, tiles)
        given = fa1[part].astype(F32).reshape(tiles * 16, CH)
        write(conv_t(zb, 1, m, w1) * mask[part].reshape(tiles * 16, CH) + given, gf_ref, m)
        return carry

    for copy in copies[3]:
        copy.wait()
    shell(halos[3], zb, 1)
    lax.fori_loop(0, steps, last_layer, 0)
    part_q.gather_one(core, partner)
    part_p.gather_one(core, partner)
    for step in range(max(plane.size, line.size) - 1):
        for part in (part_q, part_p):
            if step < part.first.size - 1:
                part.finish(core, partner, part.first.size - 2 - step)
    for part in (part_q, part_p):
        for copy in part.passed:
            copy.wait()


def convert(out_in, gf_in, gw_in, out, gf, one, two, wide, sems):
    copies = [pltpu.make_async_copy(out_in, out, sems.at[0]), pltpu.make_async_copy(gf_in, gf, sems.at[1])]
    for copy in copies:
        copy.start()
    cuts = 3
    size = gw_in.shape[1] // cuts
    for j, dst in enumerate((one, two)):
        for i in range(cuts):
            rows = pl.ds(i * size, size)
            wide[j, rows] = gw_in[j, rows].astype(F32)
            copies.append(pltpu.make_async_copy(wide.at[j, rows], dst.at[rows], sems.at[len(copies)]))
            copies[-1].start()
    for copy in copies:
        copy.wait()


def on_device(dims, features, occupied, weight_one, bias_one, weight_two, cotangent, neighbours, send_x, send_y):
    nx, ny, nzhi, nzlo, _ = dims
    nz, nxy = nzhi * nzlo, nx * ny
    slots, voxels, _ = features.shape
    scale = 1.0 / math.sqrt(slots * voxels * 2 * nxy * nz)
    vmem = pl.BlockSpec(memory_space=pltpu.VMEM)
    smem = pl.BlockSpec(memory_space=pltpu.SMEM)
    hbm = pl.BlockSpec(memory_space=pl.ANY)
    rows = KVOL * CH

    def halo():
        return [
            pltpu.VMEM((2, NONE + 1, PLANE, CH), BF),
            pltpu.VMEM((2, 7, PLANE, CH), BF),
            pltpu.VMEM((2, NONE + 1, 16, CH), BF),
            pltpu.VMEM((2, 2, PLANE, CH), BF),
            pltpu.VMEM((2, 2, PLANE, CH), BF),
            pltpu.VMEM((2, 2, 16, CH), BF),
            pltpu.VMEM((2, 2, 16, CH), BF),
        ]

    sem = lambda *shape: pltpu.SemaphoreType.DMA(shape)

    def part(total, n_one, n_two):
        one = total // n_one
        two = -(-one // (16 * n_two)) * 16
        bufs = [
            pltpu.VMEM((n_one, one, CH), BF),
            pltpu.VMEM((n_two * two, CH), BF),
            pltpu.VMEM((n_two, two, CH), BF),
            pltpu.VMEM((n_two * two, CH), BF),
        ]
        sizes = (n_one, n_one, n_two, n_two, n_two, n_two, n_one, n_one, n_one, n_one)
        return bufs, [sem(n) for n in sizes]

    bufs_q, sems_q = part(rows // 3, nz, nxy)
    bufs_p, sems_p = part(2 * rows // 3, nxy, nz)
    field = pltpu.VMEM((PLANE, 16, CH), BF)
    weight = pltpu.VMEM((rows, CH), BF)
    plain = pltpu.VMEM((PLANE, 16, CH), F32)
    padded = pltpu.VMEM((2, EDGE + 2, EDGE + 2, 16, 3 * CH), BF)
    lists = pltpu.VMEM((2, 16, CH), BF)
    made = pl.pallas_call(
        functools.partial(kernel, dims, scale),
        out_shape=(
            pltpu.VMEM(features.shape, BF),
            pltpu.VMEM(features.shape, BF),
            pltpu.VMEM((2, rows, CH), BF),
        ),
        in_specs=[vmem, vmem, hbm, vmem, hbm, vmem, smem, smem, smem],
        out_specs=(vmem, vmem, vmem),
        scratch_shapes=[
            weight, weight, plain, plain, plain, plain, field, field, field, field, padded, padded,
            pltpu.VMEM((2, 4, CH, 256), BF),
            lists, lists, weight, weight, weight,
            *halo(), *halo(), *halo(), *halo(),
            *bufs_q, *bufs_p,
            sem(2), sem(4, 10), sem(4, 10), sem(3), sem(3),
            *sems_q, *sems_p,
            pltpu.VMEM((rows // 3, CH), F32),
        ],
        compiler_params=pltpu.CompilerParams(
            collective_id=0, has_side_effects=True, vmem_limit_bytes=56 * 2**20
        ),
    )(
        features,
        occupied,
        weight_one.reshape(rows, CH),
        bias_one.reshape(1, CH),
        weight_two.reshape(rows, CH),
        cotangent,
        neighbours,
        send_x.reshape(2, -1),
        send_y.reshape(2, -1),
    )
    out, grad_features, one, two = pl.pallas_call(
        convert,
        out_shape=(
            jax.ShapeDtypeStruct(features.shape, BF),
            jax.ShapeDtypeStruct(features.shape, BF),
            jax.ShapeDtypeStruct((rows, CH), F32),
            jax.ShapeDtypeStruct((rows, CH), F32),
        ),
        in_specs=[vmem, vmem, vmem],
        out_specs=(hbm, hbm, hbm, hbm),
        scratch_shapes=[pltpu.VMEM((2, rows, CH), F32), sem(8)],
        compiler_params=pltpu.CompilerParams(vmem_limit_bytes=24 * 2**20),
    )(*made)
    return (out, grad_features, one.reshape(KVOL, CH, CH), two.reshape(KVOL, CH, CH))


def solution(mesh, dims=SLICE):
    in_specs = (
        P(("gx", "gy"), None, None),
        P(("gx", "gy"), None),
        P(),
        P(),
        P(),
        P(("gx", "gy"), None, None),
        P(("gx", "gy"), None),
        P(("gx", "gy"), None, None),
        P(("gx", "gy"), None, None),
    )
    out_specs = (P(("gx", "gy"), None, None), P(("gx", "gy"), None, None), P(), P())
    return jax.shard_map(
        functools.partial(on_device, dims), mesh=mesh, in_specs=in_specs, out_specs=out_specs, check_vma=False
    )
```
